128 devices in a mesh: zhi: 8 (over x, core), zlo: 16 (over z, y).
Axes of the slice: x: 4, y: 4, z: 4, core: 2. Of those that a mesh axis runs over, the one named last changes fastest.
Arguments:
- fine_feats: bfloat16 [786432, 256], P(('zhi', 'zlo')), may hold values from -18 to 18
- fine_counts: int32 [128], replicated, may hold values from 128 to 5280, as said below
- child_parent: int32 [786432], P(('zhi', 'zlo')), may hold values from 0 to 98303, as said below
- attn_gain: float32 [256], replicated, may hold values from 0.5 to 7
- qkv_weight: bfloat16 [256, 768], replicated, may hold values from -0.375 to 0.375
- out_weight: bfloat16 [256, 256], replicated, may hold values from -0.375 to 0.375
- ffn_gain: float32 [256], replicated, may hold values from 0.1 to 1.9
- fine_expand: bfloat16 [256, 1024], replicated, may hold values from -0.375 to 0.375
- fine_reduce: bfloat16 [1024, 256], replicated, may hold values from -0.1875 to 0.1875
- pool_weight: bfloat16 [256, 512], replicated, may hold values from -0.375 to 0.375
- coarse_gain: float32 [512], replicated, may hold values from 0.1 to 1.9
- coarse_expand: bfloat16 [512, 2048], replicated, may hold values from -0.25 to 0.25
- coarse_reduce: bfloat16 [2048, 512], replicated, may hold values from -0.125 to 0.125
- up_weight: bfloat16 [512, 256], replicated, may hold values from -0.25 to 0.25
Outputs:
- fine_result: bfloat16 [786432, 256], P(('zhi', 'zlo'))
- coarse_result: bfloat16 [98304, 512], P(('zhi', 'zlo'))
The draws below stay inside these ranges and needn't reach their ends.
Inputs may be any that keep to these rules, and one draw needn't show every extreme that they name: `fine_counts`: each device's live rows are the depth-10 children of a run of whole parents, in z-order; every device holds 128 or more, at most 5280, and some device holds exactly that most. `child_parent`: each parent row has 3 to 5 live children, contiguous in z-order, all on one device. Parent row P is held by device P // 768; the parents of a device's rows lie on that device or among the last 288 parent rows of the previous device in zhi+zlo order. Unused slots name the parent of their device's last live row.
All inputs are finite; a program needn't handle non-finite values.
Results may differ from the reference program's by a relative error of at most 0.009.
The reference program's roundings to bfloat16 on the way count: a program that leaves them out, or rounds other values in their place, can miss the bound.
Values may be sent and summed in bfloat16 or wider, within the bound.
No kernel may reach another device: no remote copies, remote signals or barrier semaphores. Data moves between devices by JAX's collectives and lax.ppermute only.
A program may use at most 256 MiB of HBM per device.

```python
import jax
import jax.numpy as jnp
from jax import lax

DF = 256
DC = 512
FF_FINE = 1024
FF_COARSE = 2048
HD = 32
WIN = 32
DILATION = 4
PCAP = 768
CAP = 6144
SPAN = 128
BORDER = 288
ROWS = 786432
NPAR = 98304


def octree_layout(key):
    layout_key = jax.random.fold_in(key, 101)
    excess_key, pick_key, child_key = jax.random.split(layout_key, 3)
    devices = NPAR // PCAP
    device_ids = jnp.arange(devices, dtype=jnp.int32)
    excess = jax.random.randint(excess_key, (devices,), 0, BORDER + 1)
    chosen = jax.random.randint(pick_key, (), 1, devices)
    excess = jnp.where(device_ids == chosen, BORDER, excess)
    excess = jnp.where(device_ids == chosen + 1, 0, excess)
    excess = jnp.where(device_ids == 0, 0, excess).astype(jnp.int32)
    following = jnp.concatenate([excess[1:], jnp.zeros((1,), jnp.int32)])
    parent_counts = (PCAP + excess - following).astype(jnp.int32)
    parent_first = (jnp.cumsum(parent_counts) - parent_counts).astype(jnp.int32)
    parent_ids = jnp.arange(NPAR, dtype=jnp.int32)
    in_chosen = (parent_ids >= parent_first[chosen]) & (parent_ids < parent_first[chosen] + parent_counts[chosen])
    children = jax.random.randint(child_key, (NPAR,), 3, 6)
    children = jnp.where(in_chosen, 5, children).astype(jnp.int32)
    child_end = jnp.cumsum(children).astype(jnp.int32)
    child_start = child_end - children
    fine_first = child_start[parent_first]
    fine_counts = (child_end[parent_first + parent_counts - 1] - fine_first).astype(jnp.int32)
    parent_of_pos = jnp.repeat(jnp.arange(NPAR, dtype=jnp.int32), children, total_repeat_length=ROWS)
    row_ids = jnp.arange(ROWS, dtype=jnp.int32)
    row_owner = row_ids // CAP
    row_slot = row_ids % CAP
    last_pos = fine_first[row_owner] + jnp.minimum(row_slot, fine_counts[row_owner] - 1)
    child_parent = parent_of_pos[last_pos].astype(jnp.int32)
    return (fine_counts, child_parent)


def draw_fine_counts(key, part):
    fine_counts, child_parent = octree_layout(key)
    return fine_counts


def draw_child_parent(key, part):
    fine_counts, child_parent = octree_layout(key)
    return child_parent


def draw_fine_feats(key, part):
    key = jax.random.fold_in(key, 7)
    noise_key = jax.random.fold_in(key, 0)
    values = jnp.clip(jax.random.normal(noise_key, (ROWS, DF), jnp.float32), -6.0, 6.0)
    return values.astype(jnp.bfloat16)


def draw_attn_gain(key, part):
    key = jax.random.fold_in(key, 5)
    return jax.random.uniform(key, (DF,), jnp.float32, 0.5, 1.5)


def gaussian(stream_key, extent, scale, limit, kind=jnp.bfloat16):
    return jnp.clip(scale * jax.random.normal(stream_key, extent, jnp.float32), -limit, limit).astype(kind)


def setup_inputs(seed: int = 0) -> dict:
    key_list = jax.random.split(jax.random.key(seed), 15)
    fine_feats = draw_fine_feats(jax.random.fold_in(key_list[14], 71), 0)
    fine_counts = draw_fine_counts(jax.random.fold_in(key_list[14], 71), 0)
    child_parent = draw_child_parent(jax.random.fold_in(key_list[14], 71), 0)
    attn_gain = draw_attn_gain(jax.random.fold_in(key_list[14], 71), 0)
    qkv_weight = gaussian(key_list[4], (DF, 3 * DF), DF ** -0.5, 0.375)
    out_weight = gaussian(key_list[5], (DF, DF), DF ** -0.5, 0.375)
    ffn_gain = jnp.clip(1.0 + 0.18 * jax.random.normal(key_list[6], (DF,), jnp.float32), 0.1, 1.9)
    fine_expand = gaussian(key_list[7], (DF, FF_FINE), DF ** -0.5, 0.375)
    fine_reduce = gaussian(key_list[8], (FF_FINE, DF), FF_FINE ** -0.5, 0.1875)
    pool_weight = gaussian(key_list[9], (DF, DC), DF ** -0.5, 0.375)
    coarse_gain = jnp.clip(1.0 + 0.18 * jax.random.normal(key_list[10], (DC,), jnp.float32), 0.1, 1.9)
    coarse_expand = gaussian(key_list[11], (DC, FF_COARSE), DC ** -0.5, 0.25)
    coarse_reduce = gaussian(key_list[12], (FF_COARSE, DC), FF_COARSE ** -0.5, 0.125)
    up_weight = gaussian(key_list[13], (DC, DF), DC ** -0.5, 0.25)
    return {"fine_feats": fine_feats, "fine_counts": fine_counts, "child_parent": child_parent, "attn_gain": attn_gain, "qkv_weight": qkv_weight, "out_weight": out_weight, "ffn_gain": ffn_gain, "fine_expand": fine_expand, "fine_reduce": fine_reduce, "pool_weight": pool_weight, "coarse_gain": coarse_gain, "coarse_expand": coarse_expand, "coarse_reduce": coarse_reduce, "up_weight": up_weight}


epsilon = 1e-05

def layer_norm(values, scale_gain):
    values = values.astype(jnp.float32)
    center = values - lax.optimization_barrier(jnp.mean(values, axis=-1, keepdims=True))
    spread = lax.optimization_barrier(jnp.mean(center * center, axis=-1, keepdims=True))
    return center * lax.rsqrt(spread + epsilon) * scale_gain

def attend_groups(packed):
    group_table, group_flags = packed
    group_count = group_table.shape[0]
    head_count = DF // HD
    shaped = group_table.astype(jnp.float32).reshape(group_count, WIN, DILATION, 3, head_count, HD)
    scores = jnp.einsum('gmrhd,gnrhd->grhmn', shaped[:, :, :, 0], shaped[:, :, :, 1]) * HD ** (-0.5)
    present = jnp.transpose(group_flags, (0, 2, 1))[:, :, None, None, :]
    scores = jnp.where(present, scores, -1e+30)
    row_max = lax.optimization_barrier(jnp.max(scores, axis=-1, keepdims=True))
    exp_scores = jnp.exp(scores - row_max)
    weights = (exp_scores / lax.optimization_barrier(jnp.sum(exp_scores, axis=-1, keepdims=True))).astype(jnp.bfloat16)
    attended = jnp.einsum('grhmn,gnrhd->gmrhd', weights.astype(jnp.float32), shaped[:, :, :, 2])
    return attended.astype(jnp.bfloat16).reshape(group_count, WIN, DILATION, DF)

def reference(fine_feats, fine_counts, child_parent, attn_gain, qkv_weight, out_weight, ffn_gain, fine_expand, fine_reduce, pool_weight, coarse_gain, coarse_expand, coarse_reduce, up_weight):
    row_ids = jnp.arange(ROWS, dtype=jnp.int32)
    row_owner = row_ids // CAP
    row_slot = row_ids % CAP
    starts = (jnp.cumsum(fine_counts) - fine_counts).astype(jnp.int32)
    is_live = row_slot < fine_counts[row_owner]
    positions = (starts[row_owner] + row_slot).astype(jnp.int32)
    normed = layer_norm(fine_feats, attn_gain).astype(jnp.bfloat16)
    projected = jnp.dot(normed, qkv_weight, preferred_element_type=jnp.float32).astype(jnp.bfloat16)
    cell_index = jnp.where(is_live, positions, ROWS).astype(jnp.int32)
    table = jnp.zeros((ROWS + 1, 3 * DF), jnp.bfloat16).at[cell_index].set(projected)[:ROWS]
    flags = jnp.zeros((ROWS + 1,), jnp.bool_).at[cell_index].set(is_live)[:ROWS]
    per_block = CAP // SPAN
    blocks = ROWS // (per_block * SPAN)
    table = table.reshape(blocks, per_block, WIN, DILATION, 3 * DF)
    flags = flags.reshape(blocks, per_block, WIN, DILATION)
    table_out = lax.map(attend_groups, (table, flags)).reshape(ROWS, DF)
    attended = table_out[jnp.minimum(cell_index, ROWS - 1)]
    hidden_one = fine_feats.astype(jnp.float32) + jnp.dot(attended, out_weight, preferred_element_type=jnp.float32)
    fine_normed = layer_norm(hidden_one, ffn_gain).astype(jnp.bfloat16)
    fine_hidden = jax.nn.gelu(jnp.dot(fine_normed, fine_expand, preferred_element_type=jnp.float32)).astype(jnp.bfloat16)
    hidden_two = (hidden_one + jnp.dot(fine_hidden, fine_reduce, preferred_element_type=jnp.float32)).astype(jnp.bfloat16)
    live_rows = jnp.where(is_live[:, None], hidden_two.astype(jnp.float32), jnp.float32(0.0))
    parent_sum = jax.ops.segment_sum(live_rows, child_parent, num_segments=NPAR)
    child_tally = jax.ops.segment_sum(is_live.astype(jnp.float32), child_parent, num_segments=NPAR)
    pooled = (parent_sum / child_tally[:, None]).astype(jnp.bfloat16)
    coarse = jnp.dot(pooled, pool_weight, preferred_element_type=jnp.float32)
    coarse_normed = layer_norm(coarse, coarse_gain).astype(jnp.bfloat16)
    coarse_hidden = jax.nn.gelu(jnp.dot(coarse_normed, coarse_expand, preferred_element_type=jnp.float32)).astype(jnp.bfloat16)
    coarse_result = (coarse + jnp.dot(coarse_hidden, coarse_reduce, preferred_element_type=jnp.float32)).astype(jnp.bfloat16)
    lifted = jnp.dot(coarse_result, up_weight, preferred_element_type=jnp.float32).astype(jnp.bfloat16)
    fine_result = jnp.where(is_live[:, None], hidden_two.astype(jnp.float32) + lifted[child_parent].astype(jnp.float32), jnp.float32(0.0)).astype(jnp.bfloat16)
    return (fine_result, coarse_result)
```

```python
import functools

import jax
import jax.numpy as jnp
from jax import lax
from jax.experimental import pallas as pl
from jax.experimental.pallas import tpu as pltpu
from jax.sharding import PartitionSpec as P

DF = 256
DC = 512
FF = 1024
FC = 2048
HD = 32
HEADS = DF // HD
SPAN = 128
DIL = 4
WIN = 32
PCAP = 768
BORDER = 288
CAP = 6144
MAXROWS = 5280
TILE = 512
LOCAL = PCAP + BORDER
XROWS = SPAN + 5632 + SPAN
POOLW = 192
SPREADW = 256
EPS = 1e-5
AXES = ("zhi", "zlo")

OFF, COUNT, LIMIT, BASE, GROUPS, LAST, FIRST = 0, 1, 2, 3, 4, 5, 6

VMEM = pltpu.VMEM
SMEM = pltpu.SMEM
bf16 = jnp.bfloat16
f32 = jnp.float32


def dot(a, b):
    return jnp.dot(a, b, preferred_element_type=f32)


def norm(v, gain):
    c = v - jnp.mean(v, axis=-1, keepdims=True)
    s = jnp.mean(c * c, axis=-1, keepdims=True)
    return c * lax.rsqrt(s + EPS) * gain


def gelu(u):
    h = 0.5 * u
    a = 0.7978845608028654
    t = jnp.tanh(u * (a + (a * 0.044715) * (u * u)))
    return h + h * t


def seg_max(s):
    out = []
    for t in range(2):
        y = s[:, t * 128 : (t + 1) * 128]
        lane = lax.broadcasted_iota(jnp.int32, y.shape, 1)
        for k in (1, 2, 4, 8, 16):
            y = jnp.maximum(y, jnp.take_along_axis(y, lane ^ k, axis=1))
        out.append(y)
    return jnp.concatenate(out, axis=1)


def put_rows(ref, at, rows):
    for t in range(DF // 128):
        ref[t, at, :] = rows[:, t * 128 : (t + 1) * 128]


def get_rows(ref, at):
    return jnp.concatenate([ref[t, at, :] for t in range(DF // 128)], axis=1)


def fine_groups(meta, gids, x, h, mask, gain1, wqkv, wout, gain2, wexp, wred):
    off = meta[OFF]
    starts = [SPAN - off + SPAN * g + r for g in gids for r in range(DIL)]
    xs = jnp.concatenate([get_rows(x, pl.ds(s, WIN, stride=DIL)) for s in starts], axis=0)
    normed = norm(xs, gain1[...]).astype(bf16)
    qkv = dot(normed, wqkv[...]).astype(bf16)
    hm = mask[...]
    key = lax.broadcasted_iota(jnp.int32, (1, DF), 1) % WIN
    scores = []
    for w in range(len(starts)):
        q = qkv[w * WIN : (w + 1) * WIN, :DF]
        k = qkv[w * WIN : (w + 1) * WIN, DF : 2 * DF]
        kb = jnp.concatenate([k] * HEADS, axis=0) * hm
        s = lax.dot_general(q, kb, (((1,), (1,)), ((), ())), preferred_element_type=f32)
        first = gids[w // DIL] * SPAN + w % DIL
        ok = first + key * DIL < meta[LIMIT]
        scores.append(jnp.where(ok, s * (HD**-0.5), -1e30))
    s = jnp.concatenate(scores, axis=0)
    e = jnp.exp(s - seg_max(s)).astype(bf16)
    den = dot(e, hm)
    outs = []
    for w in range(len(starts)):
        v = qkv[w * WIN : (w + 1) * WIN, 2 * DF :]
        vb = jnp.concatenate([v] * HEADS, axis=0) * hm
        outs.append(dot(e[w * WIN : (w + 1) * WIN], vb))
    att = (jnp.concatenate(outs, axis=0) / den).astype(bf16)
    h1 = xs + dot(att, wout[...])
    n2 = norm(h1, gain2[...]).astype(bf16)
    hid = gelu(dot(n2, wexp[...])).astype(bf16)
    h2 = (h1 + dot(hid, wred[...])).astype(bf16).astype(f32)
    for w, s in enumerate(starts):
        put_rows(h, pl.ds(s, WIN, stride=DIL), h2[w * WIN : (w + 1) * WIN])


def fine_kernel(meta, x_in, prev, nxt, parents, gain1, wqkv, wout, gain2, wexp, wred, h2_out, pooled_out,
                x, h, mask, sums, cnts):
    count = meta[COUNT]
    tiles = (count + TILE - 1) // TILE
    i = lax.broadcasted_iota(jnp.int32, (DF, DF), 0) // HD
    j = lax.broadcasted_iota(jnp.int32, (DF, DF), 1) // HD
    mask[...] = jnp.where(i == j, 1.0, 0.0).astype(bf16)
    put_rows(x, pl.ds(0, SPAN), prev[...].astype(f32))

    def widen(t, _):
        r = pl.multiple_of(t * TILE, TILE)
        put_rows(x, pl.ds(SPAN + r, TILE), x_in[pl.ds(r, TILE), :].astype(f32))
        return 0

    lax.fori_loop(0, tiles, widen, 0)
    put_rows(h, pl.ds(0, SPAN), nxt[...].astype(f32))
    for r in range(DIL):
        put_rows(x, pl.ds(SPAN + count + r, WIN, stride=DIL), get_rows(h, pl.ds(r, WIN, stride=DIL)))
    sums[...] = jnp.zeros_like(sums)
    cnts[...] = jnp.zeros_like(cnts)

    groups = meta[GROUPS]

    def fine(t, _):
        gids = [jnp.minimum(4 * t + g, groups - 1) for g in range(4)]
        fine_groups(meta, gids, x, h, mask, gain1, wqkv, wout, gain2, wexp, wred)
        return 0

    lax.fori_loop(0, (groups + 3) // 4, fine, 0)

    def pool(t, _):
        r = pl.multiple_of(t * TILE, TILE)
        row = lax.broadcasted_iota(jnp.int32, (TILE, 1), 0) + r
        hb = jnp.where(row < count, get_rows(h, pl.ds(SPAN + r, TILE)), 0.0).astype(bf16)
        h2_out[pl.ds(r, TILE), :] = hb
        lane = lax.broadcasted_iota(jnp.int32, (1, TILE), 1) + r
        seg = jnp.where(lane < count, parents[pl.ds(t, 1), :] - meta[BASE], -1)
        base = pl.multiple_of(((meta[FIRST + t] - meta[BASE]) // 16) * 16, 16)
        slot = lax.broadcasted_iota(jnp.int32, (POOLW, TILE), 0) + base
        hot = jnp.where(slot == seg, 1.0, 0.0).astype(bf16)
        sums[pl.ds(base, POOLW), :] += dot(hot, hb)
        cnts[pl.ds(base, POOLW), :] += dot(hot, jnp.ones((TILE, 128), bf16))
        return 0

    lax.fori_loop(0, tiles, pool, 0)
    n = jnp.maximum(cnts[0:LOCAL, :], 1.0)
    pooled_out[...] = (sums[0:LOCAL, :] / jnp.concatenate([n, n], axis=1)).astype(bf16)


def coarse_rows(pooled, wpool, gain, wexp, wred):
    c = dot(pooled, wpool[...])
    n = norm(c, gain[...]).astype(bf16)
    acc = c
    for k in range(FC // 512):
        hid = gelu(dot(n, wexp[:, k * 512 : (k + 1) * 512])).astype(bf16)
        acc = acc + dot(hid, wred[k * 512 : (k + 1) * 512, :])
    return acc.astype(bf16)


def coarse_kernel(meta, pooled, h2, parents, wpool, gain, wexp, wred, wup, fine_out, coarse_out, lifted):
    count = meta[COUNT]
    tiles = (count + TILE - 1) // TILE
    step = LOCAL // 3
    lifted[LOCAL : LOCAL + SPREADW, :] = jnp.zeros((SPREADW, DF), bf16)
    for t in range(3):
        res = coarse_rows(pooled[t * step : (t + 1) * step, :], wpool, gain, wexp, wred)
        lo = max(BORDER, t * step)
        coarse_out[lo - BORDER : (t + 1) * step - BORDER, :] = res[lo - t * step :]
        lifted[t * step : (t + 1) * step, :] = dot(res, wup[...]).astype(bf16)

    def spread(t, _):
        r = pl.multiple_of(t * TILE, TILE)
        lane = lax.broadcasted_iota(jnp.int32, (1, TILE), 1) + r
        base = pl.multiple_of(((meta[FIRST + t] - meta[BASE]) // 16) * 16, 16)
        seg = jnp.where(lane < count, parents[pl.ds(t, 1), :] - meta[BASE] - base, -1)
        col = jnp.transpose(jnp.broadcast_to(seg.astype(f32), (8, TILE)))[:, 0:1]
        slot = lax.broadcasted_iota(jnp.int32, (TILE, SPREADW), 1).astype(f32)
        hot = jnp.where(slot == col, 1.0, 0.0).astype(bf16)
        up = dot(hot, lifted[pl.ds(base, SPREADW), :])
        fine_out[pl.ds(r, TILE), :] = (h2[pl.ds(r, TILE), :].astype(f32) + up).astype(bf16)
        return 0

    lax.fori_loop(0, tiles, spread, 0)

    def clear(t, _):
        r = pl.multiple_of(t * TILE, TILE)
        fine_out[pl.ds(r, TILE), :] = jnp.zeros((TILE, DF), bf16)
        return 0

    lax.fori_loop(tiles, CAP // TILE, clear, 0)


def border_kernel(meta, result_in, pooled, wpool, gain, wexp, wred, result, old, pw, ew, rw, sem):
    first = meta[LAST] + 1

    @pl.when(first < PCAP)
    def _():
        loads = [pltpu.make_async_copy(a, b, sem.at[i])
                 for i, (a, b) in enumerate(((wpool, pw), (wexp, ew), (wred, rw)))]
        for c in loads:
            c.start()
        rows = result.at[pl.ds(PCAP - BORDER, BORDER)]
        get = pltpu.make_async_copy(rows, old, sem.at[3])
        get.start()
        for c in loads:
            c.wait()
        get.wait()
        row = lax.broadcasted_iota(jnp.int32, (BORDER, 1), 0) + (PCAP - BORDER)
        res = coarse_rows(pooled[...], pw, gain, ew, rw)
        old[...] = jnp.where(row >= first, res.astype(f32), old[...].astype(f32)).astype(bf16)
        put = pltpu.make_async_copy(old, rows, sem.at[3])
        put.start()
        put.wait()


def passed_along(value, steps):
    count = lax.axis_size(AXES)
    first, last = max(0, -steps), min(count, count - steps)
    return lax.ppermute(value, AXES, [(s, s + steps) for s in range(first, last)])


def body(feats, counts, parent, gain1, wqkv, wout, gain2, wexp, wred, wpool, gainc, cexp, cred, wup):
    device = lax.axis_index(AXES)
    ids = jnp.arange(counts.shape[0], dtype=jnp.int32)
    start = jnp.sum(jnp.where(ids < device, counts, 0))
    count = counts[device]
    total = jnp.sum(counts)
    off = start % SPAN
    parents = parent.reshape(CAP // TILE, TILE)
    last = parent[count - 1] - PCAP * device
    meta = jnp.concatenate([
        jnp.stack([off, count, total - start + off, PCAP * device - BORDER, (off + count + SPAN - 1) // SPAN, last]),
        parents[:, 0],
    ]).astype(jnp.int32)
    nxt = passed_along(feats[:SPAN], -1)
    prev = passed_along(lax.dynamic_slice_in_dim(feats, count - SPAN, SPAN, 0), 1)
    g1, g2, gc = gain1.reshape(1, DF), gain2.reshape(1, DF), gainc.reshape(1, DC)

    params = pltpu.CompilerParams(vmem_limit_bytes=60 * 1024 * 1024)
    vm = pl.BlockSpec(memory_space=VMEM)
    sm = pl.BlockSpec(memory_space=SMEM)
    hbm = pl.BlockSpec(memory_space=pl.ANY)

    h2, pooled = pl.pallas_call(
        fine_kernel,
        name="fine",
        out_shape=(jax.ShapeDtypeStruct((CAP, DF), bf16), jax.ShapeDtypeStruct((LOCAL, DF), bf16)),
        in_specs=[sm] + [vm] * 10,
        out_specs=(vm, vm),
        scratch_shapes=[
            VMEM((DF // 128, XROWS, 128), f32),
            VMEM((DF // 128, XROWS, 128), f32),
            VMEM((DF, DF), bf16),
            VMEM((LOCAL + POOLW, DF), f32),
            VMEM((LOCAL + POOLW, 128), f32),
        ],
        compiler_params=params,
    )(meta, feats, prev, nxt, parents, g1, wqkv, wout, g2, wexp, wred)

    incoming = passed_along(pooled[:BORDER], -1)

    fine_result, coarse_result = pl.pallas_call(
        coarse_kernel,
        name="coarse",
        out_shape=(jax.ShapeDtypeStruct((CAP, DF), bf16), jax.ShapeDtypeStruct((PCAP, DC), bf16)),
        in_specs=[sm] + [vm] * 8,
        out_specs=(vm, vm),
        scratch_shapes=[VMEM((LOCAL + SPREADW, DF), bf16)],
        compiler_params=params,
    )(meta, pooled, h2, parents, wpool, gc, cexp, cred, wup)

    coarse_result = pl.pallas_call(
        border_kernel,
        name="border",
        out_shape=jax.ShapeDtypeStruct((PCAP, DC), bf16),
        in_specs=[sm, hbm, vm, hbm, vm, hbm, hbm],
        out_specs=hbm,
        scratch_shapes=[
            VMEM((BORDER, DC), bf16),
            VMEM((DF, DC), bf16),
            VMEM((DC, FC), bf16),
            VMEM((FC, DC), bf16),
            pltpu.SemaphoreType.DMA((4,)),
        ],
        input_output_aliases={1: 0},
        compiler_params=params,
    )(meta, coarse_result, incoming, wpool, gc, cexp, cred)
    return fine_result, coarse_result


def solution(mesh):
    rows = P(AXES, None)
    in_specs = (rows, P(), P(AXES)) + (P(),) * 11
    return jax.shard_map(body, mesh=mesh, in_specs=in_specs, out_specs=(rows, rows), check_vma=False)
```

```python
import jax
import jax.numpy as jnp
from jax import lax
from jax.experimental import pallas as pl
from jax.experimental.pallas import tpu as pltpu
from jax.sharding import PartitionSpec as P

DF = 256
DC = 512
FF = 1024
FC = 2048
HD = 32
SPAN = 128
DIL = 4
WIN = 32
PCAP = 768
BORDER = 288
CAP = 6144
TILE = 512
TILES = CAP // TILE
NG = 4
LOCAL = PCAP + BORDER
STEP = 352
SLOTS = LOCAL + STEP
XROWS = SPAN + 5632 + SPAN
TAIL = 144
POOLW = 192
SPREADW = 256
BSTEP = 144
EPS = 1e-5
AXES = ("zhi", "zlo")

COUNT, LOW, HIGH, BASE, FIRST = 0, 1, 2, 3, 4
META = FIRST + TILES

VMEM = pltpu.VMEM
SMEM = pltpu.SMEM
bf16 = jnp.bfloat16
f32 = jnp.float32
i32 = jnp.int32


def dot(a, b):
    return jnp.dot(a, b, preferred_element_type=f32)


def norm(v, gain):
    c = v - jnp.mean(v, axis=-1, keepdims=True)
    s = jnp.mean(c * c, axis=-1, keepdims=True)
    return c * lax.rsqrt(s + EPS) * gain


def gelu(u):
    h = 0.5 * u
    a = 0.7978845608028654
    t = jnp.tanh(u * (a + (a * 0.044715) * (u * u)))
    return h + h * t


def put_rows(ref, at, rows):
    for t in range(DF // 128):
        ref[t, at, :] = rows[:, t * 128 : (t + 1) * 128]


def get_rows(ref, at):
    return jnp.concatenate([ref[t, at, :] for t in range(DF // 128)], axis=1)


def attend(qkv, group, limit):
    key = lax.broadcasted_iota(i32, (WIN, 1), 0) * DIL
    lb = lax.broadcasted_iota(i32, (1, DF), 1) // HD

    def one(c):
        return jnp.where(c, 1.0, 0.0).astype(bf16)

    even, odd = one(lb % 2 == 0), one(lb % 2 == 1)
    low, high = one(lb % 4 < 2), one(lb % 4 >= 2)
    first = lb % 4 < 2
    head = lax.broadcasted_iota(i32, (WIN, 128), 1) // HD
    zero = jnp.zeros((128, 128), bf16)
    weights = [None] * DIL
    for p in range(DIL // 2):
        qa, ka, _ = [qkv[2 * p * WIN : (2 * p + 1) * WIN, c * DF : (c + 1) * DF] for c in range(3)]
        qb, kb, _ = [qkv[(2 * p + 1) * WIN : (2 * p + 2) * WIN, c * DF : (c + 1) * DF] for c in range(3)]
        ab = qa * even + qb * odd
        ba = qb * even + qa * odd
        parts = [ab * low, ab * high, ba * low, ba * high]
        left = jnp.concatenate([v[:, :128] for v in parts], axis=0)
        right = jnp.concatenate([v[:, 128:] for v in parts], axis=0)
        queries = jnp.concatenate(
            [jnp.concatenate([left, zero], axis=1), jnp.concatenate([zero, right], axis=1)], axis=0
        )
        keys = jnp.concatenate([ka * even, ka * odd, kb * even, kb * odd], axis=0)
        o = lax.dot_general(keys, queries, (((1,), (1,)), ((), ())), preferred_element_type=f32)
        sa = jnp.where(first, o[0:32], o[32:64])
        sb = jnp.where(first, o[96:128], o[64:96])
        for r, s in ((2 * p, sa), (2 * p + 1, sb)):
            live = group * SPAN + r + key < limit
            s = jnp.where(live, s * (HD**-0.5), -1e30)
            e = jnp.exp(s - jnp.max(s, axis=0, keepdims=True))
            weights[r] = (e * (1.0 / jnp.sum(e, axis=0, keepdims=True))).astype(bf16)
    weights = jnp.concatenate(weights, axis=0)
    zero = jnp.zeros((64, 128), bf16)
    out = [[None] * 2 for _ in range(DIL)]
    for t in range(2):
        turned = jnp.transpose(weights[:, t * 128 : (t + 1) * 128])
        v = qkv[:, 2 * DF + t * 128 : 2 * DF + (t + 1) * 128]
        values = jnp.concatenate(
            [jnp.concatenate([v[:64], zero], axis=1), jnp.concatenate([zero, v[64:]], axis=1)], axis=0
        )
        o = dot(jnp.concatenate([turned * even[:, :128], turned * odd[:, :128]], axis=0), values)
        for r in range(DIL):
            b = o[(r % 2) * 128 : (r % 2 + 1) * 128, (r // 2) * 128 : (r // 2 + 1) * 128]
            order = (0, 2, 1, 3) if r % 2 == 0 else (2, 0, 3, 1)
            a = b[order[0] * WIN : (order[0] + 1) * WIN]
            for h in range(1, 4):
                a = jnp.where(head == h, b[order[h] * WIN : (order[h] + 1) * WIN], a)
            out[r][t] = a
    return jnp.concatenate([jnp.concatenate(o, axis=1) for o in out], axis=0).astype(bf16)


def attention_stage(off, limit, gids, x, h1s, gain, wqkv, wout):
    starts = [SPAN - off + SPAN * g + r for g in gids for r in range(DIL)]
    xs = jnp.concatenate([get_rows(x, pl.ds(s, WIN, stride=DIL)) for s in starts], axis=0)
    qkv = dot(norm(xs, gain[...]).astype(bf16), wqkv[...]).astype(bf16)
    yield
    for i, g in enumerate(gids):
        rows = slice(i * SPAN, (i + 1) * SPAN)
        h1s[rows, :] = xs[rows] + dot(attend(qkv[rows], g, limit), wout[...])
        yield


def feed_stage(off, gids, h, h1s, gain, wexp, wred):
    acc = h1s[...]
    n = norm(acc, gain[...]).astype(bf16)
    yield
    width = FF // NG
    for c in range(NG):
        u = dot(n, wexp[:, c * width : (c + 1) * width])
        acc = acc + dot(gelu(u).astype(bf16), wred[c * width : (c + 1) * width, :])
        yield
    h2 = acc.astype(bf16).astype(f32)
    starts = [SPAN - off + SPAN * g + r for g in gids for r in range(DIL)]
    for w, s in enumerate(starts):
        put_rows(h, pl.ds(s, WIN, stride=DIL), h2[w * WIN : (w + 1) * WIN])


def interleave(*stages):
    stages = list(stages)
    while stages:
        for s in list(stages):
            if next(s, stages) is stages:
                stages.remove(s)


def fine_kernel(counts, parent, feats, prev, nxt, parents, gain1, wqkv, wout, gain2, wexp, wred,
                meta, h2_out, pooled_out, x, h, h1s, xb, hb, sums, cnts, sem_in, sem_out):
    device = lax.axis_index(AXES)
    count = counts[device]
    tiles = (count + TILE - 1) // TILE

    def copy_in(t):
        rows = pl.ds(pl.multiple_of(t * TILE, TILE), TILE)
        return pltpu.make_async_copy(feats.at[rows], xb.at[rows], sem_in.at[t])

    def copy_out(t):
        rows = pl.ds(pl.multiple_of(t * TILE, TILE), TILE)
        return pltpu.make_async_copy(hb.at[rows], h2_out.at[rows], sem_out.at[t])

    def begin(t, _):
        copy_in(t).start()
        return 0

    lax.fori_loop(0, tiles, begin, 0)

    def add(i, c):
        return c[0] + jnp.where(i < device, counts[i], 0), c[1] + counts[i]

    start, total = lax.fori_loop(0, counts.shape[0], add, (jnp.int32(0), jnp.int32(0)))
    off = lax.rem(start, SPAN)
    limit = total - start + off
    groups = (off + count + SPAN - 1) // SPAN
    base0 = PCAP * device - BORDER
    meta[COUNT] = count
    meta[LOW] = parent[0] - base0
    meta[HIGH] = parent[count - 1] - base0
    meta[BASE] = base0
    for t in range(TILES):
        meta[FIRST + t] = parent[t * TILE] - base0

    put_rows(h, pl.ds(0, TAIL), prev[...].astype(f32))
    put_rows(h, pl.ds(SPAN + TAIL, SPAN), nxt[...].astype(f32))
    before = counts[jnp.maximum(device - 1, 0)] - SPAN
    skip = lax.rem(before, 16)
    for r in range(DIL):
        put_rows(x, pl.ds(r, WIN, stride=DIL), get_rows(h, pl.ds(skip + r, WIN, stride=DIL)))
    sums[...] = jnp.zeros_like(sums)
    cnts[...] = jnp.zeros_like(cnts)

    def widen(t, _):
        r = pl.multiple_of(t * TILE, TILE)
        copy_in(t).wait()
        put_rows(x, pl.ds(SPAN + r, TILE), xb[pl.ds(r, TILE), :].astype(f32))
        return 0

    lax.fori_loop(0, tiles, widen, 0)
    for r in range(DIL):
        put_rows(x, pl.ds(SPAN + count + r, WIN, stride=DIL), get_rows(h, pl.ds(SPAN + TAIL + r, WIN, stride=DIL)))

    def gids(t):
        return [jnp.minimum(NG * t + g, groups - 1) for g in range(NG)]

    def attention(t):
        return attention_stage(off, limit, gids(t), x, h1s, gain1, wqkv, wout)

    def feed(t):
        return feed_stage(off, gids(t), h, h1s, gain2, wexp, wred)

    interleave(attention(0))

    def both(t, _):
        interleave(feed(t - 1), attention(t))
        return 0

    steps = (groups + NG - 1) // NG
    lax.fori_loop(1, steps, both, 0)
    interleave(feed(steps - 1))

    def pool(t, _):
        r = pl.multiple_of(t * TILE, TILE)
        row = lax.broadcasted_iota(i32, (TILE, 1), 0) + r
        rows = jnp.where(row < count, get_rows(h, pl.ds(SPAN + r, TILE)), 0.0).astype(bf16)
        hb[pl.ds(r, TILE), :] = rows
        copy_out(t).start()
        lane = lax.broadcasted_iota(i32, (1, TILE), 1) + r
        seg = jnp.where(lane < count, parents[pl.ds(t, 1), :] - base0, -1)
        base = pl.multiple_of(((parent[r] - base0) // 16) * 16, 16)
        slot = lax.broadcasted_iota(i32, (POOLW, TILE), 0) + base
        hot = jnp.where(slot == seg, 1.0, 0.0).astype(bf16)
        sums[pl.ds(base, POOLW), :] += dot(hot, rows)
        cnts[pl.ds(base, POOLW), :] += dot(hot, jnp.ones((TILE, 128), bf16))
        return 0

    lax.fori_loop(0, tiles, pool, 0)
    n = jnp.maximum(cnts[...], 1.0)
    pooled_out[...] = (sums[...] / jnp.concatenate([n, n], axis=1)).astype(bf16)

    def end(t, _):
        copy_out(t).wait()
        return 0

    lax.fori_loop(0, tiles, end, 0)


def coarse_rows(pooled, wpool, gain, wexp, wred):
    c = dot(pooled, wpool[...])
    n = norm(c, gain[...]).astype(bf16)
    acc = c
    for k in range(FC // 512):
        hid = gelu(dot(n, wexp[:, k * 512 : (k + 1) * 512])).astype(bf16)
        acc = acc + dot(hid, wred[k * 512 : (k + 1) * 512, :])
    return acc.astype(bf16)


def coarse_kernel(meta, pooled, h2, parents, wpool, gain, cexp, cred, wup,
                  fine_out, coarse_out, lifted, res, ew, rw, hb, zeros, sem_in, sem_out, sem):
    count = meta[COUNT]
    tiles = (count + TILE - 1) // TILE

    def rows_of(t):
        return pl.ds(pl.multiple_of(t * TILE, TILE), TILE)

    def copy_in(t):
        return pltpu.make_async_copy(h2.at[rows_of(t)], hb.at[rows_of(t)], sem_in.at[t])

    def copy_out(t):
        return pltpu.make_async_copy(hb.at[rows_of(t)], fine_out.at[rows_of(t)], sem_out.at[t])

    def copy_zero(t):
        return pltpu.make_async_copy(zeros, fine_out.at[rows_of(t)], sem_out.at[t])

    loads = [pltpu.make_async_copy(a, b, sem.at[i]) for i, (a, b) in enumerate(((cexp, ew), (cred, rw)))]
    for c in loads:
        c.start()

    def begin(t, _):
        copy_in(t).start()
        return 0

    lax.fori_loop(0, tiles, begin, 0)
    zeros[...] = jnp.zeros_like(zeros)

    def clear(t, _):
        copy_zero(t).start()
        return 0

    lax.fori_loop(tiles, TILES, clear, 0)
    lifted[...] = jnp.zeros_like(lifted)
    for c in loads:
        c.wait()

    low = pl.multiple_of((meta[LOW] // 16) * 16, 16)

    def coarse(i, _):
        at = pl.ds(pl.multiple_of(low + i * STEP, 16), STEP)
        r = coarse_rows(pooled[at, :], wpool, gain, ew, rw)
        res[at, :] = r
        lifted[at, :] = dot(r, wup[...]).astype(bf16)
        return 0

    lax.fori_loop(0, (meta[HIGH] - low) // STEP + 1, coarse, 0)
    store = pltpu.make_async_copy(res.at[pl.ds(BORDER, PCAP)], coarse_out, sem.at[2])
    store.start()

    def spread(t, _):
        r = pl.multiple_of(t * TILE, TILE)
        copy_in(t).wait()
        lane = lax.broadcasted_iota(i32, (1, TILE), 1) + r
        base = pl.multiple_of((meta[FIRST + t] // 16) * 16, 16)
        seg = jnp.where(lane < count, parents[pl.ds(t, 1), :] - (meta[BASE] + base), -1)
        col = jnp.transpose(jnp.broadcast_to(seg.astype(f32), (8, TILE)))[:, 0:1]
        slot = lax.broadcasted_iota(i32, (TILE, SPREADW), 1).astype(f32)
        hot = jnp.where(slot == col, 1.0, 0.0).astype(bf16)
        up = dot(hot, lifted[pl.ds(base, SPREADW), :])
        hb[pl.ds(r, TILE), :] = (hb[pl.ds(r, TILE), :].astype(f32) + up).astype(bf16)
        copy_out(t).start()
        return 0

    lax.fori_loop(0, tiles, spread, 0)

    def end(t, _):
        copy_out(t).wait()
        return 0

    lax.fori_loop(0, tiles, end, 0)

    def end_zero(t, _):
        copy_zero(t).wait()
        return 0

    lax.fori_loop(tiles, TILES, end_zero, 0)
    store.wait()


def border_kernel(meta, result_in, pooled, wpool, gain, cexp, cred, result, old, pw, ew, rw, sem):
    first = meta[HIGH] - BORDER + 1

    @pl.when(first < PCAP)
    def _():
        loads = [pltpu.make_async_copy(a, b, sem.at[i])
                 for i, (a, b) in enumerate(((wpool, pw), (cexp, ew), (cred, rw)))]
        for c in loads:
            c.start()
        rows = result.at[pl.ds(PCAP - BORDER, BORDER)]
        get = pltpu.make_async_copy(rows, old, sem.at[3])
        get.start()
        for c in loads:
            c.wait()
        get.wait()

        def block(t, _):
            at = pl.ds(pl.multiple_of(t * BSTEP, 16), BSTEP)
            row = lax.broadcasted_iota(i32, (BSTEP, 1), 0) + (PCAP - BORDER) + t * BSTEP
            res = coarse_rows(pooled[at, :], pw, gain, ew, rw)
            old[at, :] = jnp.where(row >= first, res.astype(f32), old[at, :].astype(f32)).astype(bf16)
            return 0

        lax.fori_loop((first - (PCAP - BORDER)) // BSTEP, BORDER // BSTEP, block, 0)
        put = pltpu.make_async_copy(old, rows, sem.at[3])
        put.start()
        put.wait()


def tail_kernel(counts, feats, tail, sem):
    count = counts[lax.axis_index(AXES)]
    start = pl.multiple_of(((count - SPAN) // 16) * 16, 16)
    copy = pltpu.make_async_copy(feats.at[pl.ds(start, TAIL)], tail, sem)
    copy.start()
    copy.wait()


def passed_along(value, steps):
    count = lax.axis_size(AXES)
    first, last = max(0, -steps), min(count, count - steps)
    return lax.ppermute(value, AXES, [(s, s + steps) for s in range(first, last)])


def body(feats, counts, parent, gain1, wqkv, wout, gain2, wexp, wred, wpool, gainc, cexp, cred, wup):
    vm = pl.BlockSpec(memory_space=VMEM)
    sm = pl.BlockSpec(memory_space=SMEM)
    hbm = pl.BlockSpec(memory_space=pl.ANY)
    dma = pltpu.SemaphoreType.DMA
    params = pltpu.CompilerParams(vmem_limit_bytes=60 * 1024 * 1024)

    nxt = passed_along(feats[:SPAN], -1)
    tail = pl.pallas_call(
        tail_kernel,
        name="tail",
        out_shape=jax.ShapeDtypeStruct((TAIL, DF), bf16),
        in_specs=[sm, hbm],
        out_specs=hbm,
        scratch_shapes=[dma],
    )(counts, feats)
    prev = passed_along(tail, 1)
    parents = parent.reshape(TILES, TILE)
    g1, g2, gc = gain1.reshape(1, DF), gain2.reshape(1, DF), gainc.reshape(1, DC)

    meta, h2, pooled = pl.pallas_call(
        fine_kernel,
        name="fine",
        out_shape=(
            jax.ShapeDtypeStruct((META,), i32),
            jax.ShapeDtypeStruct((CAP, DF), bf16),
            jax.ShapeDtypeStruct((SLOTS, DF), bf16),
        ),
        in_specs=[sm, sm, hbm] + [vm] * 9,
        out_specs=(sm, hbm, vm),
        scratch_shapes=[
            VMEM((DF // 128, XROWS, 128), f32),
            VMEM((DF // 128, XROWS, 128), f32),
            VMEM((NG * SPAN, DF), f32),
            VMEM((CAP, DF), bf16),
            VMEM((CAP, DF), bf16),
            VMEM((SLOTS, DF), f32),
            VMEM((SLOTS, 128), f32),
            dma((TILES,)),
            dma((TILES,)),
        ],
        compiler_params=params,
    )(counts, parent, feats, prev, nxt, parents, g1, wqkv, wout, g2, wexp, wred)

    incoming = passed_along(pooled[:BORDER], -1)

    fine_result, coarse_result = pl.pallas_call(
        coarse_kernel,
        name="coarse",
        out_shape=(jax.ShapeDtypeStruct((CAP, DF), bf16), jax.ShapeDtypeStruct((PCAP, DC), bf16)),
        in_specs=[sm, vm, hbm, vm, vm, vm, hbm, hbm, vm],
        out_specs=(hbm, hbm),
        scratch_shapes=[
            VMEM((SLOTS, DF), bf16),
            VMEM((SLOTS, DC), bf16),
            VMEM((DC, FC), bf16),
            VMEM((FC, DC), bf16),
            VMEM((CAP, DF), bf16),
            VMEM((TILE, DF), bf16),
            dma((TILES,)),
            dma((TILES,)),
            dma((3,)),
        ],
        compiler_params=params,
    )(meta, pooled, h2, parents, wpool, gc, cexp, cred, wup)

    coarse_result = pl.pallas_call(
        border_kernel,
        name="border",
        out_shape=jax.ShapeDtypeStruct((PCAP, DC), bf16),
        in_specs=[sm, hbm, vm, hbm, vm, hbm, hbm],
        out_specs=hbm,
        scratch_shapes=[
            VMEM((BORDER, DC), bf16),
            VMEM((DF, DC), bf16),
            VMEM((DC, FC), bf16),
            VMEM((FC, DC), bf16),
            dma((4,)),
        ],
        input_output_aliases={1: 0},
        compiler_params=params,
    )(meta, coarse_result, incoming, wpool, gc, cexp, cred)
    return fine_result, coarse_result


def solution(mesh):
    rows = P(AXES, None)
    in_specs = (rows, P(), P(AXES)) + (P(),) * 11
    return jax.shard_map(body, mesh=mesh, in_specs=in_specs, out_specs=(rows, rows), check_vma=False)
```

```python
import jax
import jax.numpy as jnp
from jax import lax
from jax.experimental import pallas as pl
from jax.experimental.pallas import tpu as pltpu
from jax.sharding import PartitionSpec as P

DF = 256
DC = 512
FF = 1024
FC = 2048
HD = 32
SPAN = 128
DIL = 4
WIN = 32
PCAP = 768
BORDER = 288
CAP = 6144
TILE = 512
TILES = CAP // TILE
NG = 4
LOCAL = PCAP + BORDER
STEP = 528
SLOTS = LOCAL + STEP
XROWS = SPAN + 5632 + SPAN
TAIL = 144
POOLW = 192
SPREADW = 256
GANG = 4
BSTEP = 144
EPS = 1e-5
AXES = ("zhi", "zlo")

COUNT, LOW, HIGH, BASE, FIRST = 0, 1, 2, 3, 4
META = FIRST + TILES

VMEM = pltpu.VMEM
SMEM = pltpu.SMEM
bf16 = jnp.bfloat16
f32 = jnp.float32
i32 = jnp.int32


def dot(a, b):
    return jnp.dot(a, b, preferred_element_type=f32)


def norm(v, gain):
    c = v - jnp.mean(v, axis=-1, keepdims=True)
    s = jnp.mean(c * c, axis=-1, keepdims=True)
    return c * lax.rsqrt(s + EPS) * gain


def gelu(u):
    h = 0.5 * u
    a = 0.7978845608028654
    t = jnp.tanh(u * (a + (a * 0.044715) * (u * u)))
    return h + h * t


def place():
    return lax.axis_index(AXES)


def put_rows(ref, at, rows):
    for t in range(DF // 128):
        ref[t, at, :] = rows[:, t * 128 : (t + 1) * 128]


def get_rows(ref, at):
    return jnp.concatenate([ref[t, at, :] for t in range(DF // 128)], axis=1)


def lane_masks():
    lb = lax.broadcasted_iota(i32, (1, DF), 1) // HD

    def one(c):
        return jnp.where(c, 1.0, 0.0).astype(bf16)

    return one(lb % 2 == 0), one(lb % 2 == 1), one(lb % 4 < 2), one(lb % 4 >= 2), lb % 4 < 2


def attend_weights(qkv, group, limit):
    key = lax.broadcasted_iota(i32, (WIN, 1), 0) * DIL
    even, odd, low, high, first = lane_masks()
    zero = jnp.zeros((128, 128), bf16)
    weights = [None] * DIL
    for p in range(DIL // 2):
        qa, ka, _ = [qkv[2 * p * WIN : (2 * p + 1) * WIN, c * DF : (c + 1) * DF] for c in range(3)]
        qb, kb, _ = [qkv[(2 * p + 1) * WIN : (2 * p + 2) * WIN, c * DF : (c + 1) * DF] for c in range(3)]
        ab = qa * even + qb * odd
        ba = qb * even + qa * odd
        parts = [ab * low, ab * high, ba * low, ba * high]
        left = jnp.concatenate([v[:, :128] for v in parts], axis=0)
        right = jnp.concatenate([v[:, 128:] for v in parts], axis=0)
        queries = jnp.concatenate(
            [jnp.concatenate([left, zero], axis=1), jnp.concatenate([zero, right], axis=1)], axis=0
        )
        keys = jnp.concatenate([ka * even, ka * odd, kb * even, kb * odd], axis=0)
        o = lax.dot_general(keys, queries, (((1,), (1,)), ((), ())), preferred_element_type=f32)
        sa = jnp.where(first, o[0:32], o[32:64])
        sb = jnp.where(first, o[96:128], o[64:96])
        for r, s in ((2 * p, sa), (2 * p + 1, sb)):
            live = group * SPAN + r + key < limit
            s = jnp.where(live, s * (HD**-0.5), -1e30)
            e = jnp.exp(s - jnp.max(s, axis=0, keepdims=True))
            weights[r] = (e * (1.0 / jnp.sum(e, axis=0, keepdims=True))).astype(bf16)
    return jnp.concatenate(weights, axis=0)


def attend_values(weights, qkv):
    even, odd, _, _, _ = lane_masks()
    head = lax.broadcasted_iota(i32, (WIN, 128), 1) // HD
    zero = jnp.zeros((64, 128), bf16)
    out = [[None] * 2 for _ in range(DIL)]
    for t in range(2):
        turned = jnp.transpose(weights[:, t * 128 : (t + 1) * 128])
        v = qkv[:, 2 * DF + t * 128 : 2 * DF + (t + 1) * 128]
        values = jnp.concatenate(
            [jnp.concatenate([v[:64], zero], axis=1), jnp.concatenate([zero, v[64:]], axis=1)], axis=0
        )
        o = dot(jnp.concatenate([turned * even[:, :128], turned * odd[:, :128]], axis=0), values)
        for r in range(DIL):
            b = o[(r % 2) * 128 : (r % 2 + 1) * 128, (r // 2) * 128 : (r // 2 + 1) * 128]
            order = (0, 2, 1, 3) if r % 2 == 0 else (2, 0, 3, 1)
            a = b[order[0] * WIN : (order[0] + 1) * WIN]
            for h in range(1, 4):
                a = jnp.where(head == h, b[order[h] * WIN : (order[h] + 1) * WIN], a)
            out[r][t] = a
    return jnp.concatenate([jnp.concatenate(o, axis=1) for o in out], axis=0).astype(bf16)


def attention_stage(off, limit, gids, x, h1s, gain, wqkv, wout):
    starts = [SPAN - off + SPAN * g + r for g in gids for r in range(DIL)]
    xs = jnp.concatenate([get_rows(x, pl.ds(s, WIN, stride=DIL)) for s in starts], axis=0)
    qkv = dot(norm(xs, gain[...]).astype(bf16), wqkv[...]).astype(bf16)
    yield
    spans = [qkv[i * SPAN : (i + 1) * SPAN] for i in range(len(gids))]
    weights = []
    for v, g in zip(spans, gids):
        weights.append(attend_weights(v, g, limit))
        yield
    out = []
    for i in range(len(gids)):
        out.append(attend_values(weights[i], spans[i]))
        yield
    h1s[...] = xs + dot(jnp.concatenate(out, axis=0), wout[...])


def feed_stage(off, gids, h, h1s, gain, wexp, wred):
    acc = h1s[...]
    n = norm(acc, gain[...]).astype(bf16)
    yield
    width = FF // 2
    for c in range(2):
        u = dot(n, wexp[:, c * width : (c + 1) * width])
        yield
        u = gelu(u).astype(bf16)
        yield
        acc = acc + dot(u, wred[c * width : (c + 1) * width, :])
        yield
    h2 = acc.astype(bf16).astype(f32)
    starts = [SPAN - off + SPAN * g + r for g in gids for r in range(DIL)]
    for w, s in enumerate(starts):
        put_rows(h, pl.ds(s, WIN, stride=DIL), h2[w * WIN : (w + 1) * WIN])


def interleave(*stages):
    stages = list(stages)
    while stages:
        for s in list(stages):
            if next(s, stages) is stages:
                stages.remove(s)


def fine_kernel(counts, parent, feats, prev, nxt, parents, gain1, wqkv, wout, gain2, wexp, wred,
                meta, h2_out, pooled_out, x, h, h1s, xb, hb, sums, cnts, sem_in, sem_out):
    device = place()
    count = counts[device]
    tiles = (count + TILE - 1) // TILE

    def copy_in(t):
        rows = pl.ds(pl.multiple_of(t * TILE, TILE), TILE)
        return pltpu.make_async_copy(feats.at[rows], xb.at[rows], sem_in.at[t])

    def copy_out(t):
        rows = pl.ds(pl.multiple_of(t * TILE, TILE), TILE)
        return pltpu.make_async_copy(hb.at[rows], h2_out.at[rows], sem_out.at[t])

    def begin(t, _):
        copy_in(t).start()
        return 0

    lax.fori_loop(0, tiles, begin, 0)

    def add(i, c):
        return c[0] + jnp.where(i < device, counts[i], 0), c[1] + counts[i]

    start, total = lax.fori_loop(0, counts.shape[0], add, (jnp.int32(0), jnp.int32(0)))
    off = lax.rem(start, SPAN)
    limit = total - start + off
    groups = (off + count + SPAN - 1) // SPAN
    base0 = PCAP * device - BORDER
    meta[COUNT] = count
    meta[LOW] = parent[0] - base0
    meta[HIGH] = parent[count - 1] - base0
    meta[BASE] = base0
    for t in range(TILES):
        meta[FIRST + t] = parent[t * TILE] - base0

    put_rows(h, pl.ds(0, TAIL), prev[...].astype(f32))
    put_rows(h, pl.ds(SPAN + TAIL, SPAN), nxt[...].astype(f32))
    before = counts[jnp.maximum(device - 1, 0)] - SPAN
    skip = lax.rem(before, 16)
    for r in range(DIL):
        put_rows(x, pl.ds(r, WIN, stride=DIL), get_rows(h, pl.ds(skip + r, WIN, stride=DIL)))
    sums[...] = jnp.zeros_like(sums)
    cnts[...] = jnp.zeros_like(cnts)

    def widen(t, _):
        r = pl.multiple_of(t * TILE, TILE)
        copy_in(t).wait()
        put_rows(x, pl.ds(SPAN + r, TILE), xb[pl.ds(r, TILE), :].astype(f32))
        return 0

    lax.fori_loop(0, tiles, widen, 0)
    for r in range(DIL):
        put_rows(x, pl.ds(SPAN + count + r, WIN, stride=DIL), get_rows(h, pl.ds(SPAN + TAIL + r, WIN, stride=DIL)))

    def gids(t):
        return [jnp.minimum(NG * t + g, groups - 1) for g in range(NG)]

    def attention(t):
        return attention_stage(off, limit, gids(t), x, h1s, gain1, wqkv, wout)

    def feed(t):
        return feed_stage(off, gids(t), h, h1s, gain2, wexp, wred)

    interleave(attention(0))

    def both(t, _):
        interleave(feed(t - 1), attention(t))
        return 0

    steps = (groups + NG - 1) // NG
    lax.fori_loop(1, steps, both, 0)
    interleave(feed(steps - 1))

    def pool(t, _):
        r = pl.multiple_of(t * TILE, TILE)
        row = lax.broadcasted_iota(i32, (TILE, 1), 0) + r
        rows = jnp.where(row < count, get_rows(h, pl.ds(SPAN + r, TILE)), 0.0).astype(bf16)
        hb[pl.ds(r, TILE), :] = rows
        copy_out(t).start()
        lane = lax.broadcasted_iota(i32, (1, TILE), 1) + r
        seg = jnp.where(lane < count, parents[pl.ds(t, 1), :] - base0, -1)
        base = pl.multiple_of(((parent[r] - base0) // 16) * 16, 16)
        slot = lax.broadcasted_iota(i32, (POOLW, TILE), 0) + base
        hot = jnp.where(slot == seg, 1.0, 0.0).astype(bf16)
        sums[pl.ds(base, POOLW), :] += dot(hot, rows)
        cnts[pl.ds(base, POOLW), :] += dot(hot, jnp.ones((TILE, 128), bf16))
        return 0

    lax.fori_loop(0, tiles, pool, 0)
    n = jnp.maximum(cnts[...], 1.0)
    pooled_out[...] = (sums[...] / jnp.concatenate([n, n], axis=1)).astype(bf16)

    def end(t, _):
        copy_out(t).wait()
        return 0

    lax.fori_loop(0, tiles, end, 0)


def coarse_rows(pooled, wpool, gain, wexp, wred):
    c = dot(pooled, wpool[...])
    n = norm(c, gain[...]).astype(bf16)
    acc = c
    for k in range(FC // 512):
        hid = gelu(dot(n, wexp[:, k * 512 : (k + 1) * 512])).astype(bf16)
        acc = acc + dot(hid, wred[k * 512 : (k + 1) * 512, :])
    return acc.astype(bf16)


def coarse_kernel(meta, pooled, h2, parents, wpool, gain, cexp, cred, wup,
                  fine_out, coarse_out, lifted, res, hb, ob, zeros, sem_in, sem_out, sem):
    count = meta[COUNT]
    tiles = (count + TILE - 1) // TILE

    def rows_of(t):
        return pl.ds(pl.multiple_of(t * TILE, TILE), TILE)

    def copy_in(t):
        return pltpu.make_async_copy(h2.at[rows_of(t)], hb.at[rows_of(t)], sem_in.at[t])

    def copy_out(t):
        return pltpu.make_async_copy(ob.at[rows_of(t)], fine_out.at[rows_of(t)], sem_out.at[t])

    def copy_zero(t):
        return pltpu.make_async_copy(zeros, fine_out.at[rows_of(t)], sem_out.at[t])

    def begin(t, _):
        copy_in(t).start()
        return 0

    lax.fori_loop(0, tiles, begin, 0)
    zeros[...] = jnp.zeros_like(zeros)

    def clear(t, _):
        copy_zero(t).start()
        return 0

    lax.fori_loop(tiles, TILES, clear, 0)
    lifted[...] = jnp.zeros_like(lifted)

    low = pl.multiple_of((meta[LOW] // 16) * 16, 16)

    def coarse(i, _):
        at = pl.ds(pl.multiple_of(low + i * STEP, 16), STEP)
        r = coarse_rows(pooled[at, :], wpool, gain, cexp, cred)
        res[at, :] = r
        lifted[at, :] = dot(r, wup[...]).astype(bf16)
        return 0

    lax.fori_loop(0, (meta[HIGH] - low) // STEP + 1, coarse, 0)
    store = pltpu.make_async_copy(res.at[pl.ds(BORDER, PCAP)], coarse_out, sem)
    store.start()

    def arrived(t, _):
        copy_in(t).wait()
        return 0

    lax.fori_loop(0, tiles, arrived, 0)

    def spread(t):
        r = pl.multiple_of(t * TILE, TILE)
        lane = lax.broadcasted_iota(i32, (1, TILE), 1) + r
        base = pl.multiple_of((meta[FIRST + t] // 16) * 16, 16)
        seg = jnp.where(lane < count, parents[pl.ds(t, 1), :] - (meta[BASE] + base), -1)
        col = jnp.transpose(jnp.broadcast_to(seg.astype(f32), (8, TILE)))[:, 0:1]
        slot = lax.broadcasted_iota(i32, (TILE, SPREADW), 1).astype(f32)
        hot = jnp.where(slot == col, 1.0, 0.0).astype(bf16)
        up = dot(hot, lifted[pl.ds(base, SPREADW), :])
        ob[pl.ds(r, TILE), :] = (hb[pl.ds(r, TILE), :].astype(f32) + up).astype(bf16)

    def several(i, _):
        for j in range(GANG):
            spread(jnp.minimum(i * GANG + j, tiles - 1))
        for j in range(GANG):
            @pl.when(i * GANG + j < tiles)
            def _():
                copy_out(i * GANG + j).start()
        return 0

    lax.fori_loop(0, (tiles + GANG - 1) // GANG, several, 0)

    def end(t, _):
        copy_out(t).wait()
        return 0

    lax.fori_loop(0, tiles, end, 0)

    def end_zero(t, _):
        copy_zero(t).wait()
        return 0

    lax.fori_loop(tiles, TILES, end_zero, 0)
    store.wait()


def border_kernel(meta, result_in, pooled, wpool, gain, cexp, cred, result, old, sem):
    first = meta[HIGH] - BORDER + 1

    @pl.when(first < PCAP)
    def _():
        rows = result.at[pl.ds(PCAP - BORDER, BORDER)]
        get = pltpu.make_async_copy(rows, old, sem)
        get.start()
        get.wait()

        def block(t, _):
            at = pl.ds(pl.multiple_of(t * BSTEP, 16), BSTEP)
            row = lax.broadcasted_iota(i32, (BSTEP, 1), 0) + (PCAP - BORDER) + t * BSTEP
            res = coarse_rows(pooled[at, :], wpool, gain, cexp, cred)
            old[at, :] = jnp.where(row >= first, res.astype(f32), old[at, :].astype(f32)).astype(bf16)
            return 0

        lax.fori_loop((first - (PCAP - BORDER)) // BSTEP, BORDER // BSTEP, block, 0)
        put = pltpu.make_async_copy(old, rows, sem)
        put.start()
        put.wait()


def tail_kernel(counts, feats, tail, sem):
    count = counts[place()]
    start = pl.multiple_of(((count - SPAN) // 16) * 16, 16)
    copy = pltpu.make_async_copy(feats.at[pl.ds(start, TAIL)], tail, sem)
    copy.start()
    copy.wait()


def passed_along(value, steps):
    count = lax.axis_size(AXES)
    first, last = max(0, -steps), min(count, count - steps)
    return lax.ppermute(value, AXES, [(s, s + steps) for s in range(first, last)])


def body(feats, counts, parent, gain1, wqkv, wout, gain2, wexp, wred, wpool, gainc, cexp, cred, wup):
    vm = pl.BlockSpec(memory_space=VMEM)
    sm = pl.BlockSpec(memory_space=SMEM)
    hbm = pl.BlockSpec(memory_space=pl.ANY)
    dma = pltpu.SemaphoreType.DMA
    params = pltpu.CompilerParams(vmem_limit_bytes=44 * 1024 * 1024)

    nxt = passed_along(feats[:SPAN], -1)
    tail = pl.pallas_call(
        tail_kernel,
        name="tail",
        out_shape=jax.ShapeDtypeStruct((TAIL, DF), bf16),
        in_specs=[sm, hbm],
        out_specs=vm,
        scratch_shapes=[dma],
    )(counts, pltpu.with_memory_space_constraint(feats, pltpu.HBM))
    prev = passed_along(tail, 1)
    parents = parent.reshape(TILES, TILE)
    g1, g2, gc = gain1.reshape(1, DF), gain2.reshape(1, DF), gainc.reshape(1, DC)

    wpool, cexp, cred, wup = [pltpu.with_memory_space_constraint(w, VMEM) for w in (wpool, cexp, cred, wup)]

    meta, h2, pooled = pl.pallas_call(
        fine_kernel,
        name="fine",
        out_shape=(
            jax.ShapeDtypeStruct((META,), i32),
            jax.ShapeDtypeStruct((CAP, DF), bf16),
            jax.ShapeDtypeStruct((SLOTS, DF), bf16),
        ),
        in_specs=[sm, sm, hbm] + [vm] * 9,
        out_specs=(sm, hbm, vm),
        scratch_shapes=[
            VMEM((DF // 128, XROWS, 128), f32),
            VMEM((DF // 128, XROWS, 128), f32),
            VMEM((NG * SPAN, DF), f32),
            VMEM((CAP, DF), bf16),
            VMEM((CAP, DF), bf16),
            VMEM((SLOTS, DF), f32),
            VMEM((SLOTS, 128), f32),
            dma((TILES,)),
            dma((TILES,)),
        ],
        compiler_params=params,
    )(counts, parent, feats, prev, nxt, parents, g1, wqkv, wout, g2, wexp, wred)

    incoming = passed_along(pooled[:BORDER], -1)

    fine_result, coarse_result = pl.pallas_call(
        coarse_kernel,
        name="coarse",
        out_shape=(jax.ShapeDtypeStruct((CAP, DF), bf16), jax.ShapeDtypeStruct((PCAP, DC), bf16)),
        in_specs=[sm, vm, hbm, vm, vm, vm, vm, vm, vm],
        out_specs=(hbm, hbm),
        scratch_shapes=[
            VMEM((SLOTS, DF), bf16),
            VMEM((SLOTS, DC), bf16),
            VMEM((CAP, DF), bf16),
            VMEM((CAP, DF), bf16),
            VMEM((TILE, DF), bf16),
            dma((TILES,)),
            dma((TILES,)),
            dma,
        ],
        compiler_params=params,
    )(meta, pooled, h2, parents, wpool, gc, cexp, cred, wup)

    coarse_result = pl.pallas_call(
        border_kernel,
        name="border",
        out_shape=jax.ShapeDtypeStruct((PCAP, DC), bf16),
        in_specs=[sm, hbm, vm, vm, vm, vm, vm],
        out_specs=hbm,
        scratch_shapes=[
            VMEM((BORDER, DC), bf16),
            dma,
        ],
        input_output_aliases={1: 0},
        compiler_params=params,
    )(meta, coarse_result, incoming, wpool, gc, cexp, cred)
    return fine_result, coarse_result


def solution(mesh):
    rows = P(AXES, None)
    in_specs = (rows, P(), P(AXES)) + (P(),) * 11
    return jax.shard_map(body, mesh=mesh, in_specs=in_specs, out_specs=(rows, rows), check_vma=False)
```

```python
import jax
import jax.numpy as jnp
from jax import lax
from jax.experimental import pallas as pl
from jax.experimental.pallas import tpu as pltpu
from jax.sharding import PartitionSpec as P

DF = 256
DC = 512
FF = 1024
FC = 2048
HD = 32
SPAN = 128
DIL = 4
WIN = 32
PCAP = 768
BORDER = 288
CAP = 6144
TILE = 512
TILES = CAP // TILE
NG = 4
LOCAL = PCAP + BORDER
STEP = 528
SLOTS = LOCAL + STEP
XROWS = SPAN + 5632 + SPAN
TAIL = 144
POOLW = 192
SPREADW = 256
GANG = 4
BSTEP = 144
EPS = 1e-5
AXES = ("zhi", "zlo")

COUNT, LOW, HIGH, BASE, FIRST = 0, 1, 2, 3, 4
META = FIRST + TILES

VMEM = pltpu.VMEM
SMEM = pltpu.SMEM
bf16 = jnp.bfloat16
f32 = jnp.float32
i32 = jnp.int32


def dot(a, b):
    return jnp.dot(a, b, preferred_element_type=f32)


def norm(v, gain):
    c = v - jnp.mean(v, axis=-1, keepdims=True)
    s = jnp.mean(c * c, axis=-1, keepdims=True)
    return c * lax.rsqrt(s + EPS) * gain


def gelu(u):
    h = 0.5 * u
    a = 0.7978845608028654
    t = jnp.tanh(u * (a + (a * 0.044715) * (u * u)))
    return h + h * t


def place():
    return lax.axis_index(AXES)


def put_rows(ref, at, rows):
    for t in range(DF // 128):
        ref[t, at, :] = rows[:, t * 128 : (t + 1) * 128]


def get_rows(ref, at):
    return jnp.concatenate([ref[t, at, :] for t in range(DF // 128)], axis=1)


def lane_masks():
    lb = lax.broadcasted_iota(i32, (1, DF), 1) // HD

    def one(c):
        return jnp.where(c, 1.0, 0.0).astype(bf16)

    return one(lb % 2 == 0), one(lb % 2 == 1), one(lb % 4 < 2), one(lb % 4 >= 2), lb % 4 < 2


def attend_weights(qkv, group, limit):
    key = lax.broadcasted_iota(i32, (WIN, 1), 0) * DIL
    even, odd, low, high, first = lane_masks()
    zero = jnp.zeros((128, 128), bf16)
    weights = [None] * DIL
    for p in range(DIL // 2):
        qa, ka, _ = [qkv[2 * p * WIN : (2 * p + 1) * WIN, c * DF : (c + 1) * DF] for c in range(3)]
        qb, kb, _ = [qkv[(2 * p + 1) * WIN : (2 * p + 2) * WIN, c * DF : (c + 1) * DF] for c in range(3)]
        ab = qa * even + qb * odd
        ba = qb * even + qa * odd
        parts = [ab * low, ab * high, ba * low, ba * high]
        left = jnp.concatenate([v[:, :128] for v in parts], axis=0)
        right = jnp.concatenate([v[:, 128:] for v in parts], axis=0)
        queries = jnp.concatenate(
            [jnp.concatenate([left, zero], axis=1), jnp.concatenate([zero, right], axis=1)], axis=0
        )
        keys = jnp.concatenate([ka * even, ka * odd, kb * even, kb * odd], axis=0)
        o = lax.dot_general(keys, queries, (((1,), (1,)), ((), ())), preferred_element_type=f32)
        sa = jnp.where(first, o[0:32], o[32:64])
        sb = jnp.where(first, o[96:128], o[64:96])
        for r, s in ((2 * p, sa), (2 * p + 1, sb)):
            live = group * SPAN + r + key < limit
            s = jnp.where(live, s * (HD**-0.5), -1e30)
            e = jnp.exp(s - jnp.max(s, axis=0, keepdims=True))
            weights[r] = (e * (1.0 / jnp.sum(e, axis=0, keepdims=True))).astype(bf16)
    return jnp.concatenate(weights, axis=0)


def attend_values(weights, qkv):
    even, odd, _, _, _ = lane_masks()
    head = lax.broadcasted_iota(i32, (WIN, 128), 1) // HD
    zero = jnp.zeros((64, 128), bf16)
    out = [[None] * 2 for _ in range(DIL)]
    for t in range(2):
        turned = jnp.transpose(weights[:, t * 128 : (t + 1) * 128])
        v = qkv[:, 2 * DF + t * 128 : 2 * DF + (t + 1) * 128]
        values = jnp.concatenate(
            [jnp.concatenate([v[:64], zero], axis=1), jnp.concatenate([zero, v[64:]], axis=1)], axis=0
        )
        o = dot(jnp.concatenate([turned * even[:, :128], turned * odd[:, :128]], axis=0), values)
        for r in range(DIL):
            b = o[(r % 2) * 128 : (r % 2 + 1) * 128, (r // 2) * 128 : (r // 2 + 1) * 128]
            order = (0, 2, 1, 3) if r % 2 == 0 else (2, 0, 3, 1)
            a = b[order[0] * WIN : (order[0] + 1) * WIN]
            for h in range(1, 4):
                a = jnp.where(head == h, b[order[h] * WIN : (order[h] + 1) * WIN], a)
            out[r][t] = a
    return jnp.concatenate([jnp.concatenate(o, axis=1) for o in out], axis=0).astype(bf16)


def attention_stage(off, limit, gids, x, h1s, gain, wqkv, wout):
    starts = [SPAN - off + SPAN * g + r for g in gids for r in range(DIL)]
    xs = jnp.concatenate([get_rows(x, pl.ds(s, WIN, stride=DIL)) for s in starts], axis=0)
    qkv = dot(norm(xs, gain[...]).astype(bf16), wqkv[...]).astype(bf16)
    yield
    spans = [qkv[i * SPAN : (i + 1) * SPAN] for i in range(len(gids))]
    weights = []
    for v, g in zip(spans, gids):
        weights.append(attend_weights(v, g, limit))
        yield
    out = []
    for i in range(len(gids)):
        out.append(attend_values(weights[i], spans[i]))
        yield
    h1s[...] = xs + dot(jnp.concatenate(out, axis=0), wout[...])


def feed_stage(off, gids, h, h1s, gain, wexp, wred):
    acc = h1s[...]
    n = norm(acc, gain[...]).astype(bf16)
    yield
    width = FF // 2
    for c in range(2):
        u = dot(n, wexp[:, c * width : (c + 1) * width])
        yield
        u = gelu(u).astype(bf16)
        yield
        acc = acc + dot(u, wred[c * width : (c + 1) * width, :])
        yield
    h2 = acc.astype(bf16).astype(f32)
    starts = [SPAN - off + SPAN * g + r for g in gids for r in range(DIL)]
    for w, s in enumerate(starts):
        put_rows(h, pl.ds(s, WIN, stride=DIL), h2[w * WIN : (w + 1) * WIN])


def interleave(*stages):
    stages = list(stages)
    while stages:
        for s in list(stages):
            if next(s, stages) is stages:
                stages.remove(s)


def fine_kernel(counts, parent, feats, prev, nxt, parents, gain1, gain2, wqkv_in, wout_in, wexp_in, wred_in,
                meta, h2_out, pooled_out, x, h, h1s, sums, cnts, wqkv, wout, wexp, wred, sem):
    loads = [pltpu.make_async_copy(a, b, sem.at[i]) for i, (a, b) in enumerate(
        ((wqkv_in, wqkv), (wout_in, wout), (wexp_in, wexp), (wred_in, wred)))]
    for c in loads:
        c.start()
    device = place()
    count = counts[device]
    tiles = (count + TILE - 1) // TILE

    def add(i, c):
        return c[0] + jnp.where(i < device, counts[i], 0), c[1] + counts[i]

    start, total = lax.fori_loop(0, counts.shape[0], add, (jnp.int32(0), jnp.int32(0)))
    off = lax.rem(start, SPAN)
    limit = total - start + off
    groups = (off + count + SPAN - 1) // SPAN
    base0 = PCAP * device - BORDER
    meta[COUNT] = count
    meta[LOW] = parent[0] - base0
    meta[HIGH] = parent[count - 1] - base0
    meta[BASE] = base0
    for t in range(TILES):
        meta[FIRST + t] = parent[t * TILE] - base0

    put_rows(h, pl.ds(0, TAIL), prev[...].astype(f32))
    put_rows(h, pl.ds(SPAN + TAIL, SPAN), nxt[...].astype(f32))
    before = counts[jnp.maximum(device - 1, 0)] - SPAN
    skip = lax.rem(before, 16)
    for r in range(DIL):
        put_rows(x, pl.ds(r, WIN, stride=DIL), get_rows(h, pl.ds(skip + r, WIN, stride=DIL)))
    sums[...] = jnp.zeros_like(sums)
    cnts[...] = jnp.zeros_like(cnts)

    def widen(t, _):
        r = pl.multiple_of(t * TILE, TILE)
        put_rows(x, pl.ds(SPAN + r, TILE), feats[pl.ds(r, TILE), :].astype(f32))
        return 0

    lax.fori_loop(0, tiles, widen, 0)
    for r in range(DIL):
        put_rows(x, pl.ds(SPAN + count + r, WIN, stride=DIL), get_rows(h, pl.ds(SPAN + TAIL + r, WIN, stride=DIL)))

    def gids(t):
        return [jnp.minimum(NG * t + g, groups - 1) for g in range(NG)]

    def attention(t):
        return attention_stage(off, limit, gids(t), x, h1s, gain1, wqkv, wout)

    def feed(t):
        return feed_stage(off, gids(t), h, h1s, gain2, wexp, wred)

    loads[0].wait()
    loads[1].wait()
    interleave(attention(0))
    loads[2].wait()
    loads[3].wait()

    def both(t, _):
        interleave(feed(t - 1), attention(t))
        return 0

    steps = (groups + NG - 1) // NG
    lax.fori_loop(1, steps, both, 0)
    interleave(feed(steps - 1))

    def pool(t, _):
        r = pl.multiple_of(t * TILE, TILE)
        row = lax.broadcasted_iota(i32, (TILE, 1), 0) + r
        rows = jnp.where(row < count, get_rows(h, pl.ds(SPAN + r, TILE)), 0.0).astype(bf16)
        h2_out[pl.ds(r, TILE), :] = rows
        lane = lax.broadcasted_iota(i32, (1, TILE), 1) + r
        seg = jnp.where(lane < count, parents[pl.ds(t, 1), :] - base0, -1)
        base = pl.multiple_of(((parent[r] - base0) // 16) * 16, 16)
        slot = lax.broadcasted_iota(i32, (POOLW, TILE), 0) + base
        hot = jnp.where(slot == seg, 1.0, 0.0).astype(bf16)
        sums[pl.ds(base, POOLW), :] += dot(hot, rows)
        cnts[pl.ds(base, POOLW), :] += dot(hot, jnp.ones((TILE, 128), bf16))
        return 0

    lax.fori_loop(0, tiles, pool, 0)
    n = jnp.maximum(cnts[...], 1.0)
    pooled_out[...] = (sums[...] / jnp.concatenate([n, n], axis=1)).astype(bf16)


def coarse_rows(pooled, wpool, gain, wexp, wred):
    c = dot(pooled, wpool[...])
    n = norm(c, gain[...]).astype(bf16)
    acc = c
    for k in range(FC // 512):
        hid = gelu(dot(n, wexp[:, k * 512 : (k + 1) * 512])).astype(bf16)
        acc = acc + dot(hid, wred[k * 512 : (k + 1) * 512, :])
    return acc.astype(bf16)


def coarse_kernel(meta, pooled, wpool, gain, cexp, cred, wup, res, lifted):
    lifted[...] = jnp.zeros_like(lifted)
    low = pl.multiple_of((meta[LOW] // 16) * 16, 16)

    def coarse(i, _):
        at = pl.ds(pl.multiple_of(low + i * STEP, 16), STEP)
        r = coarse_rows(pooled[at, :], wpool, gain, cexp, cred)
        res[at, :] = r
        lifted[at, :] = dot(r, wup[...]).astype(bf16)
        return 0

    lax.fori_loop(0, (meta[HIGH] - low) // STEP + 1, coarse, 0)


def spread_kernel(meta, res, lifted, incoming, h2, parents, wpool, gain, cexp, cred,
                  fine_out, coarse_out, ob, zeros, border, sem_out, sem):
    count = meta[COUNT]
    tiles = (count + TILE - 1) // TILE
    first = meta[HIGH] - BORDER + 1
    whole = PCAP - BORDER

    def rows_of(t):
        return pl.ds(pl.multiple_of(t * TILE, TILE), TILE)

    def copy_out(t):
        return pltpu.make_async_copy(ob.at[rows_of(t)], fine_out.at[rows_of(t)], sem_out.at[t])

    def copy_zero(t):
        return pltpu.make_async_copy(zeros, fine_out.at[rows_of(t)], sem_out.at[t])

    upper = pltpu.make_async_copy(res.at[pl.ds(BORDER, whole)], coarse_out.at[pl.ds(0, whole)], sem.at[0])
    upper.start()
    zeros[...] = jnp.zeros_like(zeros)

    def clear(t, _):
        copy_zero(t).start()
        return 0

    lax.fori_loop(tiles, TILES, clear, 0)

    def spread(t):
        r = pl.multiple_of(t * TILE, TILE)
        lane = lax.broadcasted_iota(i32, (1, TILE), 1) + r
        base = pl.multiple_of((meta[FIRST + t] // 16) * 16, 16)
        seg = jnp.where(lane < count, parents[pl.ds(t, 1), :] - (meta[BASE] + base), -1)
        col = jnp.transpose(jnp.broadcast_to(seg.astype(f32), (8, TILE)))[:, 0:1]
        slot = lax.broadcasted_iota(i32, (TILE, SPREADW), 1).astype(f32)
        hot = jnp.where(slot == col, 1.0, 0.0).astype(bf16)
        up = dot(hot, lifted[pl.ds(base, SPREADW), :])
        ob[pl.ds(r, TILE), :] = (h2[pl.ds(r, TILE), :].astype(f32) + up).astype(bf16)

    def several(i, _):
        for j in range(GANG):
            spread(jnp.minimum(i * GANG + j, tiles - 1))
        for j in range(GANG):
            @pl.when(i * GANG + j < tiles)
            def _():
                copy_out(i * GANG + j).start()
        return 0

    lax.fori_loop(0, (tiles + GANG - 1) // GANG, several, 0)

    def block(at, rows):
        row = lax.broadcasted_iota(i32, (rows, 1), 0) + (whole + at)
        new = coarse_rows(incoming[at : at + rows, :], wpool, gain, cexp, cred)
        old = res[PCAP + at : PCAP + at + rows, :]
        border[at : at + rows, :] = jnp.where(row >= first, new.astype(f32), old.astype(f32)).astype(bf16)

    many = first < whole + BSTEP

    @pl.when(many)
    def _():
        block(0, BORDER)

    @pl.when(jnp.logical_not(many))
    def _():
        border[0:BSTEP, :] = res[PCAP : PCAP + BSTEP, :]

    @pl.when(jnp.logical_and(jnp.logical_not(many), first < PCAP))
    def _():
        block(BSTEP, BSTEP)

    @pl.when(first >= PCAP)
    def _():
        border[BSTEP:BORDER, :] = res[PCAP + BSTEP : PCAP + BORDER, :]

    lower = pltpu.make_async_copy(border, coarse_out.at[pl.ds(whole, BORDER)], sem.at[1])
    lower.start()

    def end(t, _):
        copy_out(t).wait()
        return 0

    lax.fori_loop(0, tiles, end, 0)

    def end_zero(t, _):
        copy_zero(t).wait()
        return 0

    lax.fori_loop(tiles, TILES, end_zero, 0)
    upper.wait()
    lower.wait()


def ends_kernel(counts, feats, head, tail, sem):
    count = counts[place()]
    start = pl.multiple_of(((count - SPAN) // 16) * 16, 16)
    first = pltpu.make_async_copy(feats.at[pl.ds(0, SPAN)], head, sem.at[0])
    last = pltpu.make_async_copy(feats.at[pl.ds(start, TAIL)], tail, sem.at[1])
    first.start()
    last.start()
    first.wait()
    last.wait()


def passed_along(value, steps):
    count = lax.axis_size(AXES)
    first, last = max(0, -steps), min(count, count - steps)
    return lax.ppermute(value, AXES, [(s, s + steps) for s in range(first, last)])


def body(feats, counts, parent, gain1, wqkv, wout, gain2, wexp, wred, wpool, gainc, cexp, cred, wup):
    vm = pl.BlockSpec(memory_space=VMEM)
    sm = pl.BlockSpec(memory_space=SMEM)
    hbm = pl.BlockSpec(memory_space=pl.ANY)
    dma = pltpu.SemaphoreType.DMA
    params = pltpu.CompilerParams(vmem_limit_bytes=44 * 1024 * 1024)

    def stay(*values):
        return [pltpu.with_memory_space_constraint(v, pltpu.HBM) for v in values]

    head, tail = pl.pallas_call(
        ends_kernel,
        name="ends",
        out_shape=(jax.ShapeDtypeStruct((SPAN, DF), bf16), jax.ShapeDtypeStruct((TAIL, DF), bf16)),
        in_specs=[sm, hbm],
        out_specs=(vm, vm),
        scratch_shapes=[dma((2,))],
    )(counts, *stay(feats))
    prev = passed_along(tail, 1)
    nxt = passed_along(head, -1)
    parents = parent.reshape(TILES, TILE)
    g1, g2, gc = gain1.reshape(1, DF), gain2.reshape(1, DF), gainc.reshape(1, DC)

    wpool, cexp, cred, wup = [pltpu.with_memory_space_constraint(w, VMEM) for w in (wpool, cexp, cred, wup)]

    meta, h2, pooled = pl.pallas_call(
        fine_kernel,
        name="fine",
        out_shape=(
            jax.ShapeDtypeStruct((META,), i32),
            jax.ShapeDtypeStruct((CAP, DF), bf16),
            jax.ShapeDtypeStruct((SLOTS, DF), bf16),
        ),
        in_specs=[sm, sm] + [vm] * 6 + [hbm] * 4,
        out_specs=(sm, vm, vm),
        scratch_shapes=[
            VMEM((DF // 128, XROWS, 128), f32),
            VMEM((DF // 128, XROWS, 128), f32),
            VMEM((NG * SPAN, DF), f32),
            VMEM((SLOTS, DF), f32),
            VMEM((SLOTS, 128), f32),
            VMEM((DF, 3 * DF), bf16),
            VMEM((DF, DF), bf16),
            VMEM((DF, FF), bf16),
            VMEM((FF, DF), bf16),
            dma((4,)),
        ],
        compiler_params=params,
    )(counts, parent, feats, prev, nxt, parents, g1, g2, *stay(wqkv, wout, wexp, wred))

    incoming = passed_along(pooled[:BORDER], -1)

    res, lifted = pl.pallas_call(
        coarse_kernel,
        name="coarse",
        out_shape=(jax.ShapeDtypeStruct((SLOTS, DC), bf16), jax.ShapeDtypeStruct((SLOTS, DF), bf16)),
        in_specs=[sm] + [vm] * 6,
        out_specs=(vm, vm),
        compiler_params=params,
    )(meta, pooled, wpool, gc, cexp, cred, wup)

    fine_result, coarse_result = pl.pallas_call(
        spread_kernel,
        name="spread",
        out_shape=(jax.ShapeDtypeStruct((CAP, DF), bf16), jax.ShapeDtypeStruct((PCAP, DC), bf16)),
        in_specs=[sm] + [vm] * 9,
        out_specs=(hbm, hbm),
        scratch_shapes=[
            VMEM((CAP, DF), bf16),
            VMEM((TILE, DF), bf16),
            VMEM((BORDER, DC), bf16),
            dma((TILES,)),
            dma((2,)),
        ],
        compiler_params=params,
    )(meta, res, lifted, incoming, h2, parents, wpool, gc, cexp, cred)
    return fine_result, coarse_result


def solution(mesh):
    rows = P(AXES, None)
    in_specs = (rows, P(), P(AXES)) + (P(),) * 11
    return jax.shard_map(body, mesh=mesh, in_specs=in_specs, out_specs=(rows, rows), check_vma=False)
```

```python
import jax
import jax.numpy as jnp
from jax import lax
from jax.experimental import pallas as pl
from jax.experimental.pallas import tpu as pltpu
from jax.sharding import PartitionSpec as P

DF = 256
DC = 512
FF = 1024
FC = 2048
HD = 32
SPAN = 128
DIL = 4
WIN = 32
PCAP = 768
BORDER = 288
CAP = 6144
TILE = 512
TILES = CAP // TILE
NG = 4
LOCAL = PCAP + BORDER
STEP = 528
SLOTS = LOCAL + STEP
XROWS = SPAN + 5632 + SPAN
TAIL = 144
POOLW = 192
SPREADW = 256
GANG = 4
BSTEP = 144
EPS = 1e-5
AXES = ("zhi", "zlo")

COUNT, LOW, HIGH, BASE, FIRST = 0, 1, 2, 3, 4
META = FIRST + TILES

VMEM = pltpu.VMEM
SMEM = pltpu.SMEM
bf16 = jnp.bfloat16
f32 = jnp.float32
i32 = jnp.int32


def dot(a, b):
    return jnp.dot(a, b, preferred_element_type=f32)


def norm(v, gain):
    c = v - jnp.mean(v, axis=-1, keepdims=True)
    s = jnp.mean(c * c, axis=-1, keepdims=True)
    return c * lax.rsqrt(s + EPS) * gain


def gelu(u):
    h = 0.5 * u
    a = 0.7978845608028654
    t = jnp.tanh(u * (a + (a * 0.044715) * (u * u)))
    return h + h * t


def place():
    return lax.axis_index(AXES)


def put_rows(ref, at, rows):
    for t in range(DF // 128):
        ref[t, at, :] = rows[:, t * 128 : (t + 1) * 128]


def get_rows(ref, at):
    return jnp.concatenate([ref[t, at, :] for t in range(DF // 128)], axis=1)


def lane_masks():
    lb = lax.broadcasted_iota(i32, (1, DF), 1) // HD

    def one(c):
        return jnp.where(c, 1.0, 0.0).astype(bf16)

    return one(lb % 2 == 0), one(lb % 2 == 1), one(lb % 4 < 2), one(lb % 4 >= 2), lb % 4 < 2


def attend_weights(qkv, group, limit):
    key = lax.broadcasted_iota(i32, (WIN, 1), 0) * DIL
    even, odd, low, high, first = lane_masks()
    zero = jnp.zeros((128, 128), bf16)
    weights = [None] * DIL
    for p in range(DIL // 2):
        qa, ka, _ = [qkv[2 * p * WIN : (2 * p + 1) * WIN, c * DF : (c + 1) * DF] for c in range(3)]
        qb, kb, _ = [qkv[(2 * p + 1) * WIN : (2 * p + 2) * WIN, c * DF : (c + 1) * DF] for c in range(3)]
        ab = qa * even + qb * odd
        ba = qb * even + qa * odd
        parts = [ab * low, ab * high, ba * low, ba * high]
        left = jnp.concatenate([v[:, :128] for v in parts], axis=0)
        right = jnp.concatenate([v[:, 128:] for v in parts], axis=0)
        queries = jnp.concatenate(
            [jnp.concatenate([left, zero], axis=1), jnp.concatenate([zero, right], axis=1)], axis=0
        )
        keys = jnp.concatenate([ka * even, ka * odd, kb * even, kb * odd], axis=0)
        o = lax.dot_general(keys, queries, (((1,), (1,)), ((), ())), preferred_element_type=f32)
        sa = jnp.where(first, o[0:32], o[32:64])
        sb = jnp.where(first, o[96:128], o[64:96])
        for r, s in ((2 * p, sa), (2 * p + 1, sb)):
            live = group * SPAN + r + key < limit
            s = jnp.where(live, s * (HD**-0.5), -1e30)
            e = jnp.exp(s - jnp.max(s, axis=0, keepdims=True))
            weights[r] = (e * (1.0 / jnp.sum(e, axis=0, keepdims=True))).astype(bf16)
    return jnp.concatenate(weights, axis=0)


def attend_values(weights, qkv):
    even, odd, _, _, _ = lane_masks()
    head = lax.broadcasted_iota(i32, (WIN, 128), 1) // HD
    zero = jnp.zeros((64, 128), bf16)
    out = [[None] * 2 for _ in range(DIL)]
    for t in range(2):
        turned = jnp.transpose(weights[:, t * 128 : (t + 1) * 128])
        v = qkv[:, 2 * DF + t * 128 : 2 * DF + (t + 1) * 128]
        values = jnp.concatenate(
            [jnp.concatenate([v[:64], zero], axis=1), jnp.concatenate([zero, v[64:]], axis=1)], axis=0
        )
        o = dot(jnp.concatenate([turned * even[:, :128], turned * odd[:, :128]], axis=0), values)
        for r in range(DIL):
            b = o[(r % 2) * 128 : (r % 2 + 1) * 128, (r // 2) * 128 : (r // 2 + 1) * 128]
            order = (0, 2, 1, 3) if r % 2 == 0 else (2, 0, 3, 1)
            a = b[order[0] * WIN : (order[0] + 1) * WIN]
            for h in range(1, 4):
                a = jnp.where(head == h, b[order[h] * WIN : (order[h] + 1) * WIN], a)
            out[r][t] = a
    return jnp.concatenate([jnp.concatenate(o, axis=1) for o in out], axis=0).astype(bf16)


def attention_stage(off, limit, gids, x, h1s, gain, wqkv, wout):
    starts = [SPAN - off + SPAN * g + r for g in gids for r in range(DIL)]
    xs = jnp.concatenate([get_rows(x, pl.ds(s, WIN, stride=DIL)) for s in starts], axis=0)
    qkv = dot(norm(xs, gain[...]).astype(bf16), wqkv[...]).astype(bf16)
    yield
    spans = [qkv[i * SPAN : (i + 1) * SPAN] for i in range(len(gids))]
    weights = []
    for v, g in zip(spans, gids):
        weights.append(attend_weights(v, g, limit))
        yield
    out = []
    for i in range(len(gids)):
        out.append(attend_values(weights[i], spans[i]))
        yield
    h1s[...] = xs + dot(jnp.concatenate(out, axis=0), wout[...])


def feed_stage(off, gids, h, h1s, gain, wexp, wred):
    acc = h1s[...]
    n = norm(acc, gain[...]).astype(bf16)
    yield
    width = FF // 2
    for c in range(2):
        u = dot(n, wexp[:, c * width : (c + 1) * width])
        yield
        u = gelu(u).astype(bf16)
        yield
        acc = acc + dot(u, wred[c * width : (c + 1) * width, :])
        yield
    h2 = acc.astype(bf16).astype(f32)
    starts = [SPAN - off + SPAN * g + r for g in gids for r in range(DIL)]
    for w, s in enumerate(starts):
        put_rows(h, pl.ds(s, WIN, stride=DIL), h2[w * WIN : (w + 1) * WIN])


def interleave(*stages):
    stages = list(stages)
    while stages:
        for s in list(stages):
            if next(s, stages) is stages:
                stages.remove(s)


def fine_kernel(counts, parent, feats, prev, nxt, parents, gain1, gain2, wqkv_in, wout_in, wexp_in, wred_in,
                meta, h2_out, pooled_out, x, h, h1s, sums, cnts, wqkv, wout, wexp, wred, sem):
    loads = [pltpu.make_async_copy(a, b, sem.at[i]) for i, (a, b) in enumerate(
        ((wqkv_in, wqkv), (wout_in, wout), (wexp_in, wexp), (wred_in, wred)))]
    for c in loads:
        c.start()
    device = place()
    count = counts[device]
    tiles = (count + TILE - 1) // TILE

    def add(i, c):
        return c[0] + jnp.where(i < device, counts[i], 0), c[1] + counts[i]

    start, total = lax.fori_loop(0, counts.shape[0], add, (jnp.int32(0), jnp.int32(0)))
    off = lax.rem(start, SPAN)
    limit = total - start + off
    groups = (off + count + SPAN - 1) // SPAN
    base0 = PCAP * device - BORDER
    meta[COUNT] = count
    meta[LOW] = parent[0] - base0
    meta[HIGH] = parent[count - 1] - base0
    meta[BASE] = base0
    for t in range(TILES):
        meta[FIRST + t] = parent[t * TILE] - base0

    put_rows(h, pl.ds(0, TAIL), prev[...].astype(f32))
    put_rows(h, pl.ds(SPAN + TAIL, SPAN), nxt[...].astype(f32))
    before = counts[jnp.maximum(device - 1, 0)] - SPAN
    skip = lax.rem(before, 16)
    for r in range(DIL):
        put_rows(x, pl.ds(r, WIN, stride=DIL), get_rows(h, pl.ds(skip + r, WIN, stride=DIL)))
    sums[...] = jnp.zeros_like(sums)
    cnts[...] = jnp.zeros_like(cnts)

    def widen(t, _):
        r = pl.multiple_of(t * TILE, TILE)
        put_rows(x, pl.ds(SPAN + r, TILE), feats[pl.ds(r, TILE), :].astype(f32))
        return 0

    lax.fori_loop(0, tiles, widen, 0)
    for r in range(DIL):
        put_rows(x, pl.ds(SPAN + count + r, WIN, stride=DIL), get_rows(h, pl.ds(SPAN + TAIL + r, WIN, stride=DIL)))

    def gids(t):
        return [jnp.minimum(NG * t + g, groups - 1) for g in range(NG)]

    def attention(t):
        return attention_stage(off, limit, gids(t), x, h1s, gain1, wqkv, wout)

    def feed(t):
        return feed_stage(off, gids(t), h, h1s, gain2, wexp, wred)

    loads[0].wait()
    loads[1].wait()
    interleave(attention(0))
    loads[2].wait()
    loads[3].wait()

    def pool_stage(t):
        r = pl.multiple_of(t * TILE, TILE)
        row = lax.broadcasted_iota(i32, (TILE, 1), 0) + r
        rows = jnp.where(row < count, get_rows(h, pl.ds(SPAN + r, TILE)), 0.0).astype(bf16)
        h2_out[pl.ds(r, TILE), :] = rows
        yield
        lane = lax.broadcasted_iota(i32, (1, TILE), 1) + r
        seg = jnp.where(lane < count, parents[pl.ds(t, 1), :] - base0, -1)
        base = pl.multiple_of(((parent[r] - base0) // 16) * 16, 16)
        slot = lax.broadcasted_iota(i32, (POOLW, TILE), 0) + base
        hot = jnp.where(slot == seg, 1.0, 0.0)
        tally = jnp.sum(hot, axis=1, keepdims=True)
        yield
        sums[pl.ds(base, POOLW), :] += dot(hot.astype(bf16), rows)
        cnts[pl.ds(base, POOLW), :] += jnp.broadcast_to(tally, (POOLW, 128))

    def pool(t, _):
        interleave(pool_stage(t))
        return 0

    def both(t, _):
        interleave(feed(t - 1), attention(t))
        return 0

    def all_three(t, _):
        interleave(pool_stage(t - 3), feed(t - 1), attention(t))
        return 0

    steps = (groups + NG - 1) // NG
    lax.fori_loop(1, jnp.minimum(steps, 3), both, 0)
    lax.fori_loop(3, steps, all_three, 0)
    interleave(feed(steps - 1))
    lax.fori_loop(jnp.maximum(steps - 3, 0), tiles, pool, 0)
    n = jnp.maximum(cnts[...], 1.0)
    pooled_out[...] = (sums[...] / jnp.concatenate([n, n], axis=1)).astype(bf16)


def coarse_rows(pooled, wpool, gain, wexp, wred):
    c = dot(pooled, wpool[...])
    n = norm(c, gain[...]).astype(bf16)
    acc = c
    u = dot(n, wexp[:, 0:512])
    for k in range(FC // 512):
        hid = gelu(u).astype(bf16)
        if k < FC // 512 - 1:
            u = dot(n, wexp[:, (k + 1) * 512 : (k + 2) * 512])
        acc = acc + dot(hid, wred[k * 512 : (k + 1) * 512, :])
    return acc.astype(bf16)


def coarse_kernel(meta, pooled, wpool, gain, cexp, cred, wup, res, lifted):
    lifted[...] = jnp.zeros_like(lifted)
    low = pl.multiple_of((meta[LOW] // 16) * 16, 16)

    def coarse(i, _):
        at = pl.ds(pl.multiple_of(low + i * STEP, 16), STEP)
        r = coarse_rows(pooled[at, :], wpool, gain, cexp, cred)
        res[at, :] = r
        lifted[at, :] = dot(r, wup[...]).astype(bf16)
        return 0

    lax.fori_loop(0, (meta[HIGH] - low) // STEP + 1, coarse, 0)


def spread_kernel(meta, res, lifted, incoming, h2, parents, wpool, gain, cexp, cred,
                  fine_out, coarse_out, ob, zeros, border, sem_out, sem):
    count = meta[COUNT]
    tiles = (count + TILE - 1) // TILE
    first = meta[HIGH] - BORDER + 1
    whole = PCAP - BORDER

    def rows_of(t):
        return pl.ds(pl.multiple_of(t * TILE, TILE), TILE)

    def copy_out(t):
        return pltpu.make_async_copy(ob.at[rows_of(t)], fine_out.at[rows_of(t)], sem_out.at[t])

    def copy_zero(t):
        return pltpu.make_async_copy(zeros, fine_out.at[rows_of(t)], sem_out.at[t])

    upper = pltpu.make_async_copy(res.at[pl.ds(BORDER, whole)], coarse_out.at[pl.ds(0, whole)], sem.at[0])
    upper.start()
    zeros[...] = jnp.zeros_like(zeros)

    def clear(t, _):
        copy_zero(t).start()
        return 0

    lax.fori_loop(tiles, TILES, clear, 0)

    def spread(t):
        r = pl.multiple_of(t * TILE, TILE)
        lane = lax.broadcasted_iota(i32, (1, TILE), 1) + r
        base = pl.multiple_of((meta[FIRST + t] // 16) * 16, 16)
        seg = jnp.where(lane < count, parents[pl.ds(t, 1), :] - (meta[BASE] + base), -1)
        col = jnp.transpose(jnp.broadcast_to(seg.astype(f32), (8, TILE)))[:, 0:1]
        slot = lax.broadcasted_iota(i32, (TILE, SPREADW), 1).astype(f32).astype(bf16)
        hot = jnp.where(slot == col.astype(bf16), jnp.ones((), bf16), jnp.zeros((), bf16))
        up = dot(hot, lifted[pl.ds(base, SPREADW), :])
        ob[pl.ds(r, TILE), :] = (h2[pl.ds(r, TILE), :].astype(f32) + up).astype(bf16)

    def several(i, _):
        for j in range(GANG):
            spread(jnp.minimum(i * GANG + j, tiles - 1))
        for j in range(GANG):
            @pl.when(i * GANG + j < tiles)
            def _():
                copy_out(i * GANG + j).start()
        return 0

    lax.fori_loop(0, (tiles + GANG - 1) // GANG, several, 0)

    def block(at, rows):
        row = lax.broadcasted_iota(i32, (rows, 1), 0) + (whole + at)
        new = coarse_rows(incoming[at : at + rows, :], wpool, gain, cexp, cred)
        old = res[PCAP + at : PCAP + at + rows, :]
        border[at : at + rows, :] = jnp.where(row >= first, new.astype(f32), old.astype(f32)).astype(bf16)

    many = first < whole + BSTEP

    @pl.when(many)
    def _():
        block(0, BORDER)

    @pl.when(jnp.logical_not(many))
    def _():
        border[0:BSTEP, :] = res[PCAP : PCAP + BSTEP, :]

    @pl.when(jnp.logical_and(jnp.logical_not(many), first < PCAP))
    def _():
        block(BSTEP, BSTEP)

    @pl.when(first >= PCAP)
    def _():
        border[BSTEP:BORDER, :] = res[PCAP + BSTEP : PCAP + BORDER, :]

    lower = pltpu.make_async_copy(border, coarse_out.at[pl.ds(whole, BORDER)], sem.at[1])
    lower.start()

    def end(t, _):
        copy_out(t).wait()
        return 0

    lax.fori_loop(0, tiles, end, 0)

    def end_zero(t, _):
        copy_zero(t).wait()
        return 0

    lax.fori_loop(tiles, TILES, end_zero, 0)
    upper.wait()
    lower.wait()


def ends_kernel(counts, feats, head, tail, sem):
    count = counts[place()]
    start = pl.multiple_of(((count - SPAN) // 16) * 16, 16)
    first = pltpu.make_async_copy(feats.at[pl.ds(0, SPAN)], head, sem.at[0])
    last = pltpu.make_async_copy(feats.at[pl.ds(start, TAIL)], tail, sem.at[1])
    first.start()
    last.start()
    first.wait()
    last.wait()


def passed_along(value, steps):
    count = lax.axis_size(AXES)
    first, last = max(0, -steps), min(count, count - steps)
    return lax.ppermute(value, AXES, [(s, s + steps) for s in range(first, last)])


def body(feats, counts, parent, gain1, wqkv, wout, gain2, wexp, wred, wpool, gainc, cexp, cred, wup):
    vm = pl.BlockSpec(memory_space=VMEM)
    sm = pl.BlockSpec(memory_space=SMEM)
    hbm = pl.BlockSpec(memory_space=pl.ANY)
    dma = pltpu.SemaphoreType.DMA
    def params(mib):
        return pltpu.CompilerParams(vmem_limit_bytes=mib * 1024 * 1024)


    def stay(*values):
        return [pltpu.with_memory_space_constraint(v, pltpu.HBM) for v in values]

    head, tail = pl.pallas_call(
        ends_kernel,
        name="ends",
        out_shape=(jax.ShapeDtypeStruct((SPAN, DF), bf16), jax.ShapeDtypeStruct((TAIL, DF), bf16)),
        in_specs=[sm, hbm],
        out_specs=(vm, vm),
        scratch_shapes=[dma((2,))],
    )(counts, *stay(feats))
    prev = passed_along(tail, 1)
    nxt = passed_along(head, -1)
    parents = parent.reshape(TILES, TILE)
    g1, g2, gc = gain1.reshape(1, DF), gain2.reshape(1, DF), gainc.reshape(1, DC)

    wpool, cexp, cred, wup = [pltpu.with_memory_space_constraint(w, VMEM) for w in (wpool, cexp, cred, wup)]

    meta, h2, pooled = pl.pallas_call(
        fine_kernel,
        name="fine",
        out_shape=(
            jax.ShapeDtypeStruct((META,), i32),
            jax.ShapeDtypeStruct((CAP, DF), bf16),
            jax.ShapeDtypeStruct((SLOTS, DF), bf16),
        ),
        in_specs=[sm, sm] + [vm] * 6 + [hbm] * 4,
        out_specs=(sm, vm, vm),
        scratch_shapes=[
            VMEM((DF // 128, XROWS, 128), f32),
            VMEM((DF // 128, XROWS, 128), f32),
            VMEM((NG * SPAN, DF), f32),
            VMEM((SLOTS, DF), f32),
            VMEM((SLOTS, 128), f32),
            VMEM((DF, 3 * DF), bf16),
            VMEM((DF, DF), bf16),
            VMEM((DF, FF), bf16),
            VMEM((FF, DF), bf16),
            dma((4,)),
        ],
        compiler_params=params(32),
    )(counts, parent, feats, prev, nxt, parents, g1, g2, *stay(wqkv, wout, wexp, wred))

    incoming = passed_along(pooled[:BORDER], -1)

    res, lifted = pl.pallas_call(
        coarse_kernel,
        name="coarse",
        out_shape=(jax.ShapeDtypeStruct((SLOTS, DC), bf16), jax.ShapeDtypeStruct((SLOTS, DF), bf16)),
        in_specs=[sm] + [vm] * 6,
        out_specs=(vm, vm),
        compiler_params=params(20),
    )(meta, pooled, wpool, gc, cexp, cred, wup)

    fine_result, coarse_result = pl.pallas_call(
        spread_kernel,
        name="spread",
        out_shape=(jax.ShapeDtypeStruct((CAP, DF), bf16), jax.ShapeDtypeStruct((PCAP, DC), bf16)),
        in_specs=[sm] + [vm] * 9,
        out_specs=(hbm, hbm),
        scratch_shapes=[
            VMEM((CAP, DF), bf16),
            VMEM((TILE, DF), bf16),
            VMEM((BORDER, DC), bf16),
            dma((TILES,)),
            dma((2,)),
        ],
        compiler_params=params(20),
    )(meta, res, lifted, incoming, h2, parents, wpool, gc, cexp, cred)
    return fine_result, coarse_result


def solution(mesh):
    rows = P(AXES, None)
    in_specs = (rows, P(), P(AXES)) + (P(),) * 11
    return jax.shard_map(body, mesh=mesh, in_specs=in_specs, out_specs=(rows, rows), check_vma=False)
```

```python
import jax
import jax.numpy as jnp
from jax import lax
from jax.experimental import pallas as pl
from jax.experimental.pallas import tpu as pltpu
from jax.sharding import PartitionSpec as P

DF = 256
DC = 512
FF = 1024
FC = 2048
HD = 32
SPAN = 128
DIL = 4
WIN = 32
PCAP = 768
BORDER = 288
CAP = 6144
TILE = 512
TILES = CAP // TILE
NG = 4
LOCAL = PCAP + BORDER
STEP = 528
SLOTS = LOCAL + STEP
XROWS = SPAN + 5632 + SPAN
TAIL = 144
POOLW = 192
SPREADW = 256
GANG = 4
LIGHT = 3700
BSTEP = 144
EPS = 1e-5
AXES = ("zhi", "zlo")

COUNT, LOW, HIGH, BASE, FIRST = 0, 1, 2, 3, 4
META = FIRST + TILES

VMEM = pltpu.VMEM
SMEM = pltpu.SMEM
bf16 = jnp.bfloat16
f32 = jnp.float32
i32 = jnp.int32


def dot(a, b):
    return jnp.dot(a, b, preferred_element_type=f32)


def norm(v, gain):
    c = v - jnp.mean(v, axis=-1, keepdims=True)
    s = jnp.mean(c * c, axis=-1, keepdims=True)
    return c * lax.rsqrt(s + EPS) * gain


def gelu(u):
    h = 0.5 * u
    a = 0.7978845608028654
    t = jnp.tanh(u * (a + (a * 0.044715) * (u * u)))
    return h + h * t


def place():
    return lax.axis_index(AXES)


def put_rows(ref, at, rows):
    for t in range(DF // 128):
        ref[t, at, :] = rows[:, t * 128 : (t + 1) * 128]


def get_rows(ref, at):
    return jnp.concatenate([ref[t, at, :] for t in range(DF // 128)], axis=1)


def lane_masks():
    lb = lax.broadcasted_iota(i32, (1, DF), 1) // HD

    def one(c):
        return jnp.where(c, 1.0, 0.0).astype(bf16)

    return one(lb % 2 == 0), one(lb % 2 == 1), one(lb % 4 < 2), one(lb % 4 >= 2), lb % 4 < 2


def attend_weights(qkv, group, limit):
    key = lax.broadcasted_iota(i32, (WIN, 1), 0) * DIL
    even, odd, low, high, first = lane_masks()
    zero = jnp.zeros((128, 128), bf16)
    weights = [None] * DIL
    for p in range(DIL // 2):
        qa, ka, _ = [qkv[2 * p * WIN : (2 * p + 1) * WIN, c * DF : (c + 1) * DF] for c in range(3)]
        qb, kb, _ = [qkv[(2 * p + 1) * WIN : (2 * p + 2) * WIN, c * DF : (c + 1) * DF] for c in range(3)]
        ab = qa * even + qb * odd
        ba = qb * even + qa * odd
        parts = [ab * low, ab * high, ba * low, ba * high]
        left = jnp.concatenate([v[:, :128] for v in parts], axis=0)
        right = jnp.concatenate([v[:, 128:] for v in parts], axis=0)
        queries = jnp.concatenate(
            [jnp.concatenate([left, zero], axis=1), jnp.concatenate([zero, right], axis=1)], axis=0
        )
        keys = jnp.concatenate([ka * even, ka * odd, kb * even, kb * odd], axis=0)
        o = lax.dot_general(keys, queries, (((1,), (1,)), ((), ())), preferred_element_type=f32)
        sa = jnp.where(first, o[0:32], o[32:64])
        sb = jnp.where(first, o[96:128], o[64:96])
        for r, s in ((2 * p, sa), (2 * p + 1, sb)):
            live = group * SPAN + r + key < limit
            s = jnp.where(live, s * (HD**-0.5), -1e30)
            e = jnp.exp(s - jnp.max(s, axis=0, keepdims=True))
            weights[r] = (e * (1.0 / jnp.sum(e, axis=0, keepdims=True))).astype(bf16)
    return jnp.concatenate(weights, axis=0)


def attend_values(weights, qkv):
    even, odd, _, _, _ = lane_masks()
    head = lax.broadcasted_iota(i32, (WIN, 128), 1) // HD
    zero = jnp.zeros((64, 128), bf16)
    out = [[None] * 2 for _ in range(DIL)]
    for t in range(2):
        turned = jnp.transpose(weights[:, t * 128 : (t + 1) * 128])
        v = qkv[:, 2 * DF + t * 128 : 2 * DF + (t + 1) * 128]
        values = jnp.concatenate(
            [jnp.concatenate([v[:64], zero], axis=1), jnp.concatenate([zero, v[64:]], axis=1)], axis=0
        )
        o = dot(jnp.concatenate([turned * even[:, :128], turned * odd[:, :128]], axis=0), values)
        for r in range(DIL):
            b = o[(r % 2) * 128 : (r % 2 + 1) * 128, (r // 2) * 128 : (r // 2 + 1) * 128]
            order = (0, 2, 1, 3) if r % 2 == 0 else (2, 0, 3, 1)
            a = b[order[0] * WIN : (order[0] + 1) * WIN]
            for h in range(1, 4):
                a = jnp.where(head == h, b[order[h] * WIN : (order[h] + 1) * WIN], a)
            out[r][t] = a
    return jnp.concatenate([jnp.concatenate(o, axis=1) for o in out], axis=0).astype(bf16)


def attention_stage(off, limit, gids, x, h1s, gain, wqkv, wout):
    starts = [SPAN - off + SPAN * g + r for g in gids for r in range(DIL)]
    xs = jnp.concatenate([get_rows(x, pl.ds(s, WIN, stride=DIL)) for s in starts], axis=0)
    qkv = dot(norm(xs, gain[...]).astype(bf16), wqkv[...]).astype(bf16)
    yield
    spans = [qkv[i * SPAN : (i + 1) * SPAN] for i in range(len(gids))]
    weights = []
    for v, g in zip(spans, gids):
        weights.append(attend_weights(v, g, limit))
        yield
    out = []
    for i in range(len(gids)):
        out.append(attend_values(weights[i], spans[i]))
        yield
    h1s[...] = xs + dot(jnp.concatenate(out, axis=0), wout[...])


def feed_stage(off, gids, h, h1s, gain, wexp, wred):
    acc = h1s[...]
    n = norm(acc, gain[...]).astype(bf16)
    yield
    width = FF // 2
    for c in range(2):
        u = dot(n, wexp[:, c * width : (c + 1) * width])
        yield
        u = gelu(u).astype(bf16)
        yield
        acc = acc + dot(u, wred[c * width : (c + 1) * width, :])
        yield
    h2 = acc.astype(bf16).astype(f32)
    starts = [SPAN - off + SPAN * g + r for g in gids for r in range(DIL)]
    for w, s in enumerate(starts):
        put_rows(h, pl.ds(s, WIN, stride=DIL), h2[w * WIN : (w + 1) * WIN])


def interleave(*stages):
    stages = list(stages)
    while stages:
        for s in list(stages):
            if next(s, stages) is stages:
                stages.remove(s)


def fine_kernel(counts, parent, feats, prev, nxt, parents, gain1, gain2, gainc, wqkv_in, wout_in, wexp_in, wred_in,
                wpool_in, cexp_in, cred_in, wup_in, meta, h2_out, pooled_out, res, lifted, x, h, h1s, sums, cnts, wqkv, wout, wexp, wred,
                wpool, cexp, cred, wup, sem):
    loads = [pltpu.make_async_copy(a, b, sem.at[i]) for i, (a, b) in enumerate(
        ((wqkv_in, wqkv), (wout_in, wout), (wexp_in, wexp), (wred_in, wred)))]
    for c in loads:
        c.start()
    device = place()
    count = counts[device]
    tiles = (count + TILE - 1) // TILE
    light = count <= LIGHT
    coarse_loads = [pltpu.make_async_copy(a, b, sem.at[4 + i]) for i, (a, b) in enumerate(
        ((wpool_in, wpool), (cexp_in, cexp), (cred_in, cred), (wup_in, wup)))]

    @pl.when(light)
    def _():
        for c in coarse_loads:
            c.start()

    def add(i, c):
        return c[0] + jnp.where(i < device, counts[i], 0), c[1] + counts[i]

    start, total = lax.fori_loop(0, counts.shape[0], add, (jnp.int32(0), jnp.int32(0)))
    off = lax.rem(start, SPAN)
    limit = total - start + off
    groups = (off + count + SPAN - 1) // SPAN
    base0 = PCAP * device - BORDER
    meta[COUNT] = count
    meta[LOW] = parent[0] - base0
    meta[HIGH] = parent[count - 1] - base0
    meta[BASE] = base0
    for t in range(TILES):
        meta[FIRST + t] = parent[t * TILE] - base0

    put_rows(h, pl.ds(0, TAIL), prev[...].astype(f32))
    put_rows(h, pl.ds(SPAN + TAIL, SPAN), nxt[...].astype(f32))
    before = counts[jnp.maximum(device - 1, 0)] - SPAN
    skip = lax.rem(before, 16)
    for r in range(DIL):
        put_rows(x, pl.ds(r, WIN, stride=DIL), get_rows(h, pl.ds(skip + r, WIN, stride=DIL)))
    sums[...] = jnp.zeros_like(sums)
    cnts[...] = jnp.zeros_like(cnts)

    def widen(t, _):
        r = pl.multiple_of(t * TILE, TILE)
        put_rows(x, pl.ds(SPAN + r, TILE), feats[pl.ds(r, TILE), :].astype(f32))
        return 0

    lax.fori_loop(0, tiles, widen, 0)
    for r in range(DIL):
        put_rows(x, pl.ds(SPAN + count + r, WIN, stride=DIL), get_rows(h, pl.ds(SPAN + TAIL + r, WIN, stride=DIL)))

    def gids(t):
        return [jnp.minimum(NG * t + g, groups - 1) for g in range(NG)]

    def attention(t):
        return attention_stage(off, limit, gids(t), x, h1s, gain1, wqkv, wout)

    def feed(t):
        return feed_stage(off, gids(t), h, h1s, gain2, wexp, wred)

    loads[0].wait()
    loads[1].wait()
    interleave(attention(0))
    loads[2].wait()
    loads[3].wait()

    def pool_stage(t):
        r = pl.multiple_of(t * TILE, TILE)
        row = lax.broadcasted_iota(i32, (TILE, 1), 0) + r
        rows = jnp.where(row < count, get_rows(h, pl.ds(SPAN + r, TILE)), 0.0).astype(bf16)
        h2_out[pl.ds(r, TILE), :] = rows
        yield
        lane = lax.broadcasted_iota(i32, (1, TILE), 1) + r
        seg = jnp.where(lane < count, parents[pl.ds(t, 1), :] - base0, -1)
        base = pl.multiple_of(((parent[r] - base0) // 16) * 16, 16)
        slot = lax.broadcasted_iota(i32, (POOLW, TILE), 0) + base
        hot = jnp.where(slot == seg, 1.0, 0.0)
        tally = jnp.sum(hot, axis=1, keepdims=True)
        yield
        sums[pl.ds(base, POOLW), :] += dot(hot.astype(bf16), rows)
        cnts[pl.ds(base, POOLW), :] += jnp.broadcast_to(tally, (POOLW, 128))

    def pool(t, _):
        interleave(pool_stage(t))
        return 0

    def both(t, _):
        interleave(feed(t - 1), attention(t))
        return 0

    def all_three(t, _):
        interleave(pool_stage(t - 3), feed(t - 1), attention(t))
        return 0

    steps = (groups + NG - 1) // NG
    lax.fori_loop(1, jnp.minimum(steps, 3), both, 0)
    lax.fori_loop(3, steps, all_three, 0)
    interleave(feed(steps - 1))
    lax.fori_loop(jnp.maximum(steps - 3, 0), tiles, pool, 0)
    n = jnp.maximum(cnts[...], 1.0)
    pooled_out[...] = (sums[...] / jnp.concatenate([n, n], axis=1)).astype(bf16)

    @pl.when(light)
    def _():
        for c in coarse_loads:
            c.wait()
        coarse_parents(parent[0] - base0, parent[count - 1] - base0, pooled_out, wpool, gainc, cexp, cred, wup,
                       res, lifted)


def coarse_rows(pooled, wpool, gain, wexp, wred):
    c = dot(pooled, wpool[...])
    n = norm(c, gain[...]).astype(bf16)
    acc = c
    u = dot(n, wexp[:, 0:512])
    for k in range(FC // 512):
        hid = gelu(u).astype(bf16)
        if k < FC // 512 - 1:
            u = dot(n, wexp[:, (k + 1) * 512 : (k + 2) * 512])
        acc = acc + dot(hid, wred[k * 512 : (k + 1) * 512, :])
    return acc.astype(bf16)


def coarse_parents(first, last, pooled, wpool, gain, cexp, cred, wup, res, lifted):
    lifted[...] = jnp.zeros_like(lifted)
    low = pl.multiple_of((first // 16) * 16, 16)

    def coarse(i, _):
        at = pl.ds(pl.multiple_of(low + i * STEP, 16), STEP)
        r = coarse_rows(pooled[at, :], wpool, gain, cexp, cred)
        res[at, :] = r
        lifted[at, :] = dot(r, wup[...]).astype(bf16)
        return 0

    lax.fori_loop(0, (last - low) // STEP + 1, coarse, 0)


def coarse_kernel(meta, pooled, res_in, lifted_in, wpool, gain, cexp, cred, wup, res, lifted):
    light = meta[COUNT] <= LIGHT

    @pl.when(light)
    def _():
        res[...] = res_in[...]
        lifted[...] = lifted_in[...]

    @pl.when(jnp.logical_not(light))
    def _():
        coarse_parents(meta[LOW], meta[HIGH], pooled, wpool, gain, cexp, cred, wup, res, lifted)


def spread_kernel(meta, res, lifted, incoming, h2, parents, wpool, gain, cexp, cred,
                  fine_out, coarse_out, ob, zeros, border, sem_out, sem):
    count = meta[COUNT]
    tiles = (count + TILE - 1) // TILE
    first = meta[HIGH] - BORDER + 1
    whole = PCAP - BORDER

    def rows_of(t):
        return pl.ds(pl.multiple_of(t * TILE, TILE), TILE)

    def copy_out(t):
        return pltpu.make_async_copy(ob.at[rows_of(t)], fine_out.at[rows_of(t)], sem_out.at[t])

    def copy_zero(t):
        return pltpu.make_async_copy(zeros, fine_out.at[rows_of(t)], sem_out.at[t])

    upper = pltpu.make_async_copy(res.at[pl.ds(BORDER, whole)], coarse_out.at[pl.ds(0, whole)], sem.at[0])
    upper.start()
    zeros[...] = jnp.zeros_like(zeros)

    def clear(t, _):
        copy_zero(t).start()
        return 0

    lax.fori_loop(tiles, TILES, clear, 0)

    def spread(t):
        r = pl.multiple_of(t * TILE, TILE)
        lane = lax.broadcasted_iota(i32, (1, TILE), 1) + r
        base = pl.multiple_of((meta[FIRST + t] // 16) * 16, 16)
        seg = jnp.where(lane < count, parents[pl.ds(t, 1), :] - (meta[BASE] + base), -1)
        col = jnp.transpose(jnp.broadcast_to(seg.astype(f32), (8, TILE)))[:, 0:1]
        slot = lax.broadcasted_iota(i32, (TILE, SPREADW), 1).astype(f32).astype(bf16)
        hot = jnp.where(slot == col.astype(bf16), jnp.ones((), bf16), jnp.zeros((), bf16))
        up = dot(hot, lifted[pl.ds(base, SPREADW), :])
        ob[pl.ds(r, TILE), :] = (h2[pl.ds(r, TILE), :].astype(f32) + up).astype(bf16)

    def several(i, _):
        for j in range(GANG):
            spread(jnp.minimum(i * GANG + j, tiles - 1))
        for j in range(GANG):
            @pl.when(i * GANG + j < tiles)
            def _():
                copy_out(i * GANG + j).start()
        return 0

    lax.fori_loop(0, (tiles + GANG - 1) // GANG, several, 0)

    def block(at, rows):
        row = lax.broadcasted_iota(i32, (rows, 1), 0) + (whole + at)
        new = coarse_rows(incoming[at : at + rows, :], wpool, gain, cexp, cred)
        old = res[PCAP + at : PCAP + at + rows, :]
        border[at : at + rows, :] = jnp.where(row >= first, new.astype(f32), old.astype(f32)).astype(bf16)

    many = first < whole + BSTEP

    @pl.when(many)
    def _():
        block(0, BORDER)

    @pl.when(jnp.logical_not(many))
    def _():
        border[0:BSTEP, :] = res[PCAP : PCAP + BSTEP, :]

    @pl.when(jnp.logical_and(jnp.logical_not(many), first < PCAP))
    def _():
        block(BSTEP, BSTEP)

    @pl.when(first >= PCAP)
    def _():
        border[BSTEP:BORDER, :] = res[PCAP + BSTEP : PCAP + BORDER, :]

    lower = pltpu.make_async_copy(border, coarse_out.at[pl.ds(whole, BORDER)], sem.at[1])
    lower.start()

    def end(t, _):
        copy_out(t).wait()
        return 0

    lax.fori_loop(0, tiles, end, 0)

    def end_zero(t, _):
        copy_zero(t).wait()
        return 0

    lax.fori_loop(tiles, TILES, end_zero, 0)
    upper.wait()
    lower.wait()


def ends_kernel(counts, feats, head, tail, sem):
    count = counts[place()]
    start = pl.multiple_of(((count - SPAN) // 16) * 16, 16)
    first = pltpu.make_async_copy(feats.at[pl.ds(0, SPAN)], head, sem.at[0])
    last = pltpu.make_async_copy(feats.at[pl.ds(start, TAIL)], tail, sem.at[1])
    first.start()
    last.start()
    first.wait()
    last.wait()


def passed_along(value, steps):
    count = lax.axis_size(AXES)
    first, last = max(0, -steps), min(count, count - steps)
    return lax.ppermute(value, AXES, [(s, s + steps) for s in range(first, last)])


def body(feats, counts, parent, gain1, wqkv, wout, gain2, wexp, wred, wpool, gainc, cexp, cred, wup):
    vm = pl.BlockSpec(memory_space=VMEM)
    sm = pl.BlockSpec(memory_space=SMEM)
    hbm = pl.BlockSpec(memory_space=pl.ANY)
    dma = pltpu.SemaphoreType.DMA
    def params(mib):
        return pltpu.CompilerParams(vmem_limit_bytes=mib * 1024 * 1024)


    def stay(*values):
        return [pltpu.with_memory_space_constraint(v, pltpu.HBM) for v in values]

    head, tail = pl.pallas_call(
        ends_kernel,
        name="ends",
        out_shape=(jax.ShapeDtypeStruct((SPAN, DF), bf16), jax.ShapeDtypeStruct((TAIL, DF), bf16)),
        in_specs=[sm, hbm],
        out_specs=(vm, vm),
        scratch_shapes=[dma((2,))],
    )(counts, *stay(feats))
    prev = passed_along(tail, 1)
    nxt = passed_along(head, -1)
    parents = parent.reshape(TILES, TILE)
    g1, g2, gc = gain1.reshape(1, DF), gain2.reshape(1, DF), gainc.reshape(1, DC)

    cold = stay(wpool, cexp, cred, wup)
    wpool, cexp, cred, wup = [pltpu.with_memory_space_constraint(w, VMEM) for w in (wpool, cexp, cred, wup)]

    meta, h2, pooled, res, lifted = pl.pallas_call(
        fine_kernel,
        name="fine",
        out_shape=(
            jax.ShapeDtypeStruct((META,), i32),
            jax.ShapeDtypeStruct((CAP, DF), bf16),
            jax.ShapeDtypeStruct((SLOTS, DF), bf16),
            jax.ShapeDtypeStruct((SLOTS, DC), bf16),
            jax.ShapeDtypeStruct((SLOTS, DF), bf16),
        ),
        in_specs=[sm, sm] + [vm] * 7 + [hbm] * 8,
        out_specs=(sm, vm, vm, vm, vm),
        scratch_shapes=[
            VMEM((DF // 128, XROWS, 128), f32),
            VMEM((DF // 128, XROWS, 128), f32),
            VMEM((NG * SPAN, DF), f32),
            VMEM((SLOTS, DF), f32),
            VMEM((SLOTS, 128), f32),
            VMEM((DF, 3 * DF), bf16),
            VMEM((DF, DF), bf16),
            VMEM((DF, FF), bf16),
            VMEM((FF, DF), bf16),
            VMEM((DF, DC), bf16),
            VMEM((DC, FC), bf16),
            VMEM((FC, DC), bf16),
            VMEM((DC, DF), bf16),
            dma((8,)),
        ],
        compiler_params=params(38),
    )(counts, parent, feats, prev, nxt, parents, g1, g2, gc, *stay(wqkv, wout, wexp, wred), *cold)

    incoming = passed_along(pooled[:BORDER], -1)

    res, lifted = pl.pallas_call(
        coarse_kernel,
        name="coarse",
        out_shape=(jax.ShapeDtypeStruct((SLOTS, DC), bf16), jax.ShapeDtypeStruct((SLOTS, DF), bf16)),
        in_specs=[sm] + [vm] * 8,
        out_specs=(vm, vm),
        compiler_params=params(20),
    )(meta, pooled, res, lifted, wpool, gc, cexp, cred, wup)

    fine_result, coarse_result = pl.pallas_call(
        spread_kernel,
        name="spread",
        out_shape=(jax.ShapeDtypeStruct((CAP, DF), bf16), jax.ShapeDtypeStruct((PCAP, DC), bf16)),
        in_specs=[sm] + [vm] * 9,
        out_specs=(hbm, hbm),
        scratch_shapes=[
            VMEM((CAP, DF), bf16),
            VMEM((TILE, DF), bf16),
            VMEM((BORDER, DC), bf16),
            dma((TILES,)),
            dma((2,)),
        ],
        compiler_params=params(20),
    )(meta, res, lifted, incoming, h2, parents, wpool, gc, cexp, cred)
    return fine_result, coarse_result


def solution(mesh):
    rows = P(AXES, None)
    in_specs = (rows, P(), P(AXES)) + (P(),) * 11
    return jax.shard_map(body, mesh=mesh, in_specs=in_specs, out_specs=(rows, rows), check_vma=False)
```

```python
import jax
import jax.numpy as jnp
from jax import lax
from jax.experimental import pallas as pl
from jax.experimental.pallas import tpu as pltpu
from jax.sharding import PartitionSpec as P

DF = 256
DC = 512
FF = 1024
FC = 2048
HD = 32
SPAN = 128
DIL = 4
WIN = 32
PCAP = 768
BORDER = 288
CAP = 6144
TILE = 512
TILES = CAP // TILE
NG = 4
LOCAL = PCAP + BORDER
STEP = 528
SLOTS = LOCAL + STEP
XROWS = SPAN + 5632 + SPAN
TAIL = 144
POOLW = 192
SPREADW = 256
GANG = 4
LIGHT = 4352
BSTEP = 144
EPS = 1e-5
AXES = ("zhi", "zlo")

COUNT, LOW, HIGH, BASE, FIRST = 0, 1, 2, 3, 4
META = FIRST + TILES

VMEM = pltpu.VMEM
SMEM = pltpu.SMEM
bf16 = jnp.bfloat16
f32 = jnp.float32
i32 = jnp.int32


def dot(a, b):
    return jnp.dot(a, b, preferred_element_type=f32)


def norm(v, gain):
    c = v - jnp.mean(v, axis=-1, keepdims=True)
    s = jnp.mean(c * c, axis=-1, keepdims=True)
    return c * lax.rsqrt(s + EPS) * gain


def gelu(u):
    h = 0.5 * u
    a = 0.7978845608028654
    t = jnp.tanh(u * (a + (a * 0.044715) * (u * u)))
    return h + h * t


def place():
    return lax.axis_index(AXES)


def put_rows(ref, at, rows):
    for t in range(DF // 128):
        ref[t, at, :] = rows[:, t * 128 : (t + 1) * 128]


def get_rows(ref, at):
    return jnp.concatenate([ref[t, at, :] for t in range(DF // 128)], axis=1)


def lane_masks():
    lb = lax.broadcasted_iota(i32, (1, DF), 1) // HD

    def one(c):
        return jnp.where(c, 1.0, 0.0).astype(bf16)

    return one(lb % 2 == 0), one(lb % 2 == 1), one(lb % 4 < 2), one(lb % 4 >= 2), lb % 4 < 2


def attend_weights(qkv, group, limit):
    key = lax.broadcasted_iota(i32, (WIN, 1), 0) * DIL
    even, odd, low, high, first = lane_masks()
    zero = jnp.zeros((128, 128), bf16)
    weights = [None] * DIL
    for p in range(DIL // 2):
        qa, ka, _ = [qkv[2 * p * WIN : (2 * p + 1) * WIN, c * DF : (c + 1) * DF] for c in range(3)]
        qb, kb, _ = [qkv[(2 * p + 1) * WIN : (2 * p + 2) * WIN, c * DF : (c + 1) * DF] for c in range(3)]
        ab = qa * even + qb * odd
        ba = qb * even + qa * odd
        parts = [ab * low, ab * high, ba * low, ba * high]
        left = jnp.concatenate([v[:, :128] for v in parts], axis=0)
        right = jnp.concatenate([v[:, 128:] for v in parts], axis=0)
        queries = jnp.concatenate(
            [jnp.concatenate([left, zero], axis=1), jnp.concatenate([zero, right], axis=1)], axis=0
        )
        keys = jnp.concatenate([ka * even, ka * odd, kb * even, kb * odd], axis=0)
        o = lax.dot_general(keys, queries, (((1,), (1,)), ((), ())), preferred_element_type=f32)
        sa = jnp.where(first, o[0:32], o[32:64])
        sb = jnp.where(first, o[96:128], o[64:96])
        for r, s in ((2 * p, sa), (2 * p + 1, sb)):
            live = group * SPAN + r + key < limit
            s = jnp.where(live, s * (HD**-0.5), -1e30)
            e = jnp.exp(s - jnp.max(s, axis=0, keepdims=True))
            weights[r] = (e * (1.0 / jnp.sum(e, axis=0, keepdims=True))).astype(bf16)
    return jnp.concatenate(weights, axis=0)


def attend_values(weights, qkv):
    even, odd, _, _, _ = lane_masks()
    head = lax.broadcasted_iota(i32, (WIN, 128), 1) // HD
    zero = jnp.zeros((64, 128), bf16)
    out = [[None] * 2 for _ in range(DIL)]
    for t in range(2):
        turned = jnp.transpose(weights[:, t * 128 : (t + 1) * 128])
        v = qkv[:, 2 * DF + t * 128 : 2 * DF + (t + 1) * 128]
        values = jnp.concatenate(
            [jnp.concatenate([v[:64], zero], axis=1), jnp.concatenate([zero, v[64:]], axis=1)], axis=0
        )
        o = dot(jnp.concatenate([turned * even[:, :128], turned * odd[:, :128]], axis=0), values)
        for r in range(DIL):
            b = o[(r % 2) * 128 : (r % 2 + 1) * 128, (r // 2) * 128 : (r // 2 + 1) * 128]
            order = (0, 2, 1, 3) if r % 2 == 0 else (2, 0, 3, 1)
            a = b[order[0] * WIN : (order[0] + 1) * WIN]
            for h in range(1, 4):
                a = jnp.where(head == h, b[order[h] * WIN : (order[h] + 1) * WIN], a)
            out[r][t] = a
    return jnp.concatenate([jnp.concatenate(o, axis=1) for o in out], axis=0).astype(bf16)


def attention_stage(off, limit, gids, x, h1s, gain, wqkv, wout):
    starts = [SPAN - off + SPAN * g + r for g in gids for r in range(DIL)]
    xs = jnp.concatenate([get_rows(x, pl.ds(s, WIN, stride=DIL)) for s in starts], axis=0)
    qkv = dot(norm(xs, gain[...]).astype(bf16), wqkv[...]).astype(bf16)
    yield
    spans = [qkv[i * SPAN : (i + 1) * SPAN] for i in range(len(gids))]
    weights = []
    for v, g in zip(spans, gids):
        weights.append(attend_weights(v, g, limit))
        yield
    out = []
    for i in range(len(gids)):
        out.append(attend_values(weights[i], spans[i]))
        yield
    h1s[...] = xs + dot(jnp.concatenate(out, axis=0), wout[...])


def feed_stage(off, gids, h, h1s, gain, wexp, wred):
    acc = h1s[...]
    n = norm(acc, gain[...]).astype(bf16)
    yield
    width = FF // 2
    for c in range(2):
        u = dot(n, wexp[:, c * width : (c + 1) * width])
        yield
        u = gelu(u).astype(bf16)
        yield
        acc = acc + dot(u, wred[c * width : (c + 1) * width, :])
        yield
    h2 = acc.astype(bf16).astype(f32)
    starts = [SPAN - off + SPAN * g + r for g in gids for r in range(DIL)]
    for w, s in enumerate(starts):
        put_rows(h, pl.ds(s, WIN, stride=DIL), h2[w * WIN : (w + 1) * WIN])


def interleave(*stages):
    stages = list(stages)
    while stages:
        for s in list(stages):
            if next(s, stages) is stages:
                stages.remove(s)


def fine_kernel(counts, parent, feats, prev, nxt, parents, gain1, gain2, gainc, wqkv_in, wout_in, wexp_in, wred_in,
                wpool_in, cexp_in, cred_in, wup_in, meta, h2_out, pooled_out, res, lifted, x, h, h1s, sums, cnts, wqkv, wout, wexp, wred,
                wpool, cexp, cred, wup, sem):
    loads = [pltpu.make_async_copy(a, b, sem.at[i]) for i, (a, b) in enumerate(
        ((wqkv_in, wqkv), (wout_in, wout), (wexp_in, wexp), (wred_in, wred)))]
    for c in loads:
        c.start()
    device = place()
    count = counts[device]
    tiles = (count + TILE - 1) // TILE
    light = count <= LIGHT
    coarse_loads = [pltpu.make_async_copy(a, b, sem.at[4 + i]) for i, (a, b) in enumerate(
        ((wpool_in, wpool), (cexp_in, cexp), (cred_in, cred), (wup_in, wup)))]

    @pl.when(light)
    def _():
        for c in coarse_loads:
            c.start()

    def add(i, c):
        return c[0] + jnp.where(i < device, counts[i], 0), c[1] + counts[i]

    start, total = lax.fori_loop(0, counts.shape[0], add, (jnp.int32(0), jnp.int32(0)))
    off = lax.rem(start, SPAN)
    limit = total - start + off
    groups = (off + count + SPAN - 1) // SPAN
    base0 = PCAP * device - BORDER
    meta[COUNT] = count
    meta[LOW] = parent[0] - base0
    meta[HIGH] = parent[count - 1] - base0
    meta[BASE] = base0
    for t in range(TILES):
        meta[FIRST + t] = parent[t * TILE] - base0

    put_rows(h, pl.ds(0, TAIL), prev[...].astype(f32))
    put_rows(h, pl.ds(SPAN + TAIL, SPAN), nxt[...].astype(f32))
    before = counts[jnp.maximum(device - 1, 0)] - SPAN
    skip = lax.rem(before, 16)
    for r in range(DIL):
        put_rows(x, pl.ds(r, WIN, stride=DIL), get_rows(h, pl.ds(skip + r, WIN, stride=DIL)))
    sums[...] = jnp.zeros_like(sums)
    cnts[...] = jnp.zeros_like(cnts)

    def widen(t, _):
        r = pl.multiple_of(t * TILE, TILE)
        put_rows(x, pl.ds(SPAN + r, TILE), feats[pl.ds(r, TILE), :].astype(f32))
        return 0

    lax.fori_loop(0, tiles, widen, 0)
    for r in range(DIL):
        put_rows(x, pl.ds(SPAN + count + r, WIN, stride=DIL), get_rows(h, pl.ds(SPAN + TAIL + r, WIN, stride=DIL)))

    def gids(t):
        return [jnp.minimum(NG * t + g, groups - 1) for g in range(NG)]

    def attention(t):
        return attention_stage(off, limit, gids(t), x, h1s, gain1, wqkv, wout)

    def feed(t):
        return feed_stage(off, gids(t), h, h1s, gain2, wexp, wred)

    loads[0].wait()
    loads[1].wait()
    interleave(attention(0))
    loads[2].wait()
    loads[3].wait()

    def pool_stage(t):
        r = pl.multiple_of(t * TILE, TILE)
        row = lax.broadcasted_iota(i32, (TILE, 1), 0) + r
        rows = jnp.where(row < count, get_rows(h, pl.ds(SPAN + r, TILE)), 0.0).astype(bf16)
        h2_out[pl.ds(r, TILE), :] = rows
        yield
        lane = lax.broadcasted_iota(i32, (1, TILE), 1) + r
        seg = jnp.where(lane < count, parents[pl.ds(t, 1), :] - base0, -1)
        base = pl.multiple_of(((parent[r] - base0) // 16) * 16, 16)
        slot = lax.broadcasted_iota(i32, (POOLW, TILE), 0) + base
        hot = jnp.where(slot == seg, 1.0, 0.0)
        tally = jnp.sum(hot, axis=1, keepdims=True)
        yield
        sums[pl.ds(base, POOLW), :] += dot(hot.astype(bf16), rows)
        cnts[pl.ds(base, POOLW), :] += jnp.broadcast_to(tally, (POOLW, 128))

    def pool(t, _):
        interleave(pool_stage(t))
        return 0

    def both(t, _):
        interleave(feed(t - 1), attention(t))
        return 0

    def all_three(t, _):
        interleave(pool_stage(t - 3), feed(t - 1), attention(t))
        return 0

    steps = (groups + NG - 1) // NG
    lax.fori_loop(1, jnp.minimum(steps, 3), both, 0)
    lax.fori_loop(3, steps, all_three, 0)
    interleave(feed(steps - 1))
    lax.fori_loop(jnp.maximum(steps - 3, 0), tiles, pool, 0)
    n = jnp.maximum(cnts[...], 1.0)
    pooled_out[...] = (sums[...] / jnp.concatenate([n, n], axis=1)).astype(bf16)

    @pl.when(light)
    def _():
        for c in coarse_loads:
            c.wait()
        coarse_parents(parent[0] - base0, parent[count - 1] - base0, pooled_out, wpool, gainc, cexp, cred, wup,
                       res, lifted)


def coarse_rows(pooled, wpool, gain, wexp, wred):
    c = dot(pooled, wpool[...])
    n = norm(c, gain[...]).astype(bf16)
    acc = c
    u = dot(n, wexp[:, 0:512])
    for k in range(FC // 512):
        hid = gelu(u).astype(bf16)
        if k < FC // 512 - 1:
            u = dot(n, wexp[:, (k + 1) * 512 : (k + 2) * 512])
        acc = acc + dot(hid, wred[k * 512 : (k + 1) * 512, :])
    return acc.astype(bf16)


def coarse_parents(first, last, pooled, wpool, gain, cexp, cred, wup, res, lifted):
    lifted[...] = jnp.zeros_like(lifted)
    low = pl.multiple_of((first // 16) * 16, 16)

    def coarse(i, _):
        at = pl.ds(pl.multiple_of(low + i * STEP, 16), STEP)
        r = coarse_rows(pooled[at, :], wpool, gain, cexp, cred)
        res[at, :] = r
        lifted[at, :] = dot(r, wup[...]).astype(bf16)
        return 0

    lax.fori_loop(0, (last - low) // STEP + 1, coarse, 0)


def coarse_kernel(meta, pooled, res_in, lifted_in, wpool, gain, cexp, cred, wup, res, lifted, sem):
    light = meta[COUNT] <= LIGHT

    @pl.when(light)
    def _():
        copies = [pltpu.make_async_copy(res_in, res, sem.at[0]), pltpu.make_async_copy(lifted_in, lifted, sem.at[1])]
        for c in copies:
            c.start()
        for c in copies:
            c.wait()

    @pl.when(jnp.logical_not(light))
    def _():
        coarse_parents(meta[LOW], meta[HIGH], pooled, wpool, gain, cexp, cred, wup, res, lifted)


def spread_kernel(meta, res, lifted, incoming, h2, parents, wpool, gain, cexp, cred,
                  fine_out, coarse_out, ob, zeros, border, sem_out, sem):
    count = meta[COUNT]
    tiles = (count + TILE - 1) // TILE
    first = meta[HIGH] - BORDER + 1
    whole = PCAP - BORDER

    def rows_of(t):
        return pl.ds(pl.multiple_of(t * TILE, TILE), TILE)

    def copy_out(t):
        return pltpu.make_async_copy(ob.at[rows_of(t)], fine_out.at[rows_of(t)], sem_out.at[t])

    def copy_zero(t):
        return pltpu.make_async_copy(zeros, fine_out.at[rows_of(t)], sem_out.at[t])

    upper = pltpu.make_async_copy(res.at[pl.ds(BORDER, whole)], coarse_out.at[pl.ds(0, whole)], sem.at[0])
    upper.start()
    zeros[...] = jnp.zeros_like(zeros)

    def clear(t, _):
        copy_zero(t).start()
        return 0

    lax.fori_loop(tiles, TILES, clear, 0)

    def spread(t):
        r = pl.multiple_of(t * TILE, TILE)
        lane = lax.broadcasted_iota(i32, (1, TILE), 1) + r
        base = pl.multiple_of((meta[FIRST + t] // 16) * 16, 16)
        seg = jnp.where(lane < count, parents[pl.ds(t, 1), :] - (meta[BASE] + base), -1)
        col = jnp.transpose(jnp.broadcast_to(seg.astype(f32), (8, TILE)))[:, 0:1]
        slot = lax.broadcasted_iota(i32, (TILE, SPREADW), 1).astype(f32).astype(bf16)
        hot = jnp.where(slot == col.astype(bf16), jnp.ones((), bf16), jnp.zeros((), bf16))
        up = dot(hot, lifted[pl.ds(base, SPREADW), :])
        ob[pl.ds(r, TILE), :] = (h2[pl.ds(r, TILE), :].astype(f32) + up).astype(bf16)

    def several(i, _):
        for j in range(GANG):
            spread(jnp.minimum(i * GANG + j, tiles - 1))
        for j in range(GANG):
            @pl.when(i * GANG + j < tiles)
            def _():
                copy_out(i * GANG + j).start()
        return 0

    lax.fori_loop(0, (tiles + GANG - 1) // GANG, several, 0)

    def block(at, rows):
        row = lax.broadcasted_iota(i32, (rows, 1), 0) + (whole + at)
        new = coarse_rows(incoming[at : at + rows, :], wpool, gain, cexp, cred)
        old = res[PCAP + at : PCAP + at + rows, :]
        border[at : at + rows, :] = jnp.where(row >= first, new.astype(f32), old.astype(f32)).astype(bf16)

    many = first < whole + BSTEP

    @pl.when(many)
    def _():
        block(0, BORDER)

    @pl.when(jnp.logical_not(many))
    def _():
        border[0:BSTEP, :] = res[PCAP : PCAP + BSTEP, :]

    @pl.when(jnp.logical_and(jnp.logical_not(many), first < PCAP))
    def _():
        block(BSTEP, BSTEP)

    @pl.when(first >= PCAP)
    def _():
        border[BSTEP:BORDER, :] = res[PCAP + BSTEP : PCAP + BORDER, :]

    lower = pltpu.make_async_copy(border, coarse_out.at[pl.ds(whole, BORDER)], sem.at[1])
    lower.start()

    def end(t, _):
        copy_out(t).wait()
        return 0

    lax.fori_loop(0, tiles, end, 0)

    def end_zero(t, _):
        copy_zero(t).wait()
        return 0

    lax.fori_loop(tiles, TILES, end_zero, 0)
    upper.wait()
    lower.wait()


def ends_kernel(counts, feats, head, tail, sem):
    count = counts[place()]
    start = pl.multiple_of(((count - SPAN) // 16) * 16, 16)
    first = pltpu.make_async_copy(feats.at[pl.ds(0, SPAN)], head, sem.at[0])
    last = pltpu.make_async_copy(feats.at[pl.ds(start, TAIL)], tail, sem.at[1])
    first.start()
    last.start()
    first.wait()
    last.wait()


def passed_along(value, steps):
    count = lax.axis_size(AXES)
    first, last = max(0, -steps), min(count, count - steps)
    return lax.ppermute(value, AXES, [(s, s + steps) for s in range(first, last)])


def body(feats, counts, parent, gain1, wqkv, wout, gain2, wexp, wred, wpool, gainc, cexp, cred, wup):
    vm = pl.BlockSpec(memory_space=VMEM)
    sm = pl.BlockSpec(memory_space=SMEM)
    hbm = pl.BlockSpec(memory_space=pl.ANY)
    dma = pltpu.SemaphoreType.DMA
    def params(mib):
        return pltpu.CompilerParams(vmem_limit_bytes=mib * 1024 * 1024)


    def stay(*values):
        return [pltpu.with_memory_space_constraint(v, pltpu.HBM) for v in values]

    head, tail = pl.pallas_call(
        ends_kernel,
        name="ends",
        out_shape=(jax.ShapeDtypeStruct((SPAN, DF), bf16), jax.ShapeDtypeStruct((TAIL, DF), bf16)),
        in_specs=[sm, hbm],
        out_specs=(vm, vm),
        scratch_shapes=[dma((2,))],
    )(counts, *stay(feats))
    prev = passed_along(tail, 1)
    nxt = passed_along(head, -1)
    parents = parent.reshape(TILES, TILE)
    g1, g2, gc = gain1.reshape(1, DF), gain2.reshape(1, DF), gainc.reshape(1, DC)

    cold = stay(wpool, cexp, cred, wup)
    wpool, cexp, cred, wup = [pltpu.with_memory_space_constraint(w, VMEM) for w in (wpool, cexp, cred, wup)]

    meta, h2, pooled, res, lifted = pl.pallas_call(
        fine_kernel,
        name="fine",
        out_shape=(
            jax.ShapeDtypeStruct((META,), i32),
            jax.ShapeDtypeStruct((CAP, DF), bf16),
            jax.ShapeDtypeStruct((SLOTS, DF), bf16),
            jax.ShapeDtypeStruct((SLOTS, DC), bf16),
            jax.ShapeDtypeStruct((SLOTS, DF), bf16),
        ),
        in_specs=[sm, sm] + [vm] * 7 + [hbm] * 8,
        out_specs=(sm, vm, vm, vm, vm),
        scratch_shapes=[
            VMEM((DF // 128, XROWS, 128), f32),
            VMEM((DF // 128, XROWS, 128), f32),
            VMEM((NG * SPAN, DF), f32),
            VMEM((SLOTS, DF), f32),
            VMEM((SLOTS, 128), f32),
            VMEM((DF, 3 * DF), bf16),
            VMEM((DF, DF), bf16),
            VMEM((DF, FF), bf16),
            VMEM((FF, DF), bf16),
            VMEM((DF, DC), bf16),
            VMEM((DC, FC), bf16),
            VMEM((FC, DC), bf16),
            VMEM((DC, DF), bf16),
            dma((8,)),
        ],
        compiler_params=params(38),
    )(counts, parent, feats, prev, nxt, parents, g1, g2, gc, *stay(wqkv, wout, wexp, wred), *cold)

    incoming = passed_along(pooled[:BORDER], -1)

    res, lifted = pl.pallas_call(
        coarse_kernel,
        name="coarse",
        out_shape=(jax.ShapeDtypeStruct((SLOTS, DC), bf16), jax.ShapeDtypeStruct((SLOTS, DF), bf16)),
        in_specs=[sm, vm, hbm, hbm] + [vm] * 5,
        out_specs=(vm, vm),
        scratch_shapes=[dma((2,))],
        compiler_params=params(20),
    )(meta, pooled, res, lifted, wpool, gc, cexp, cred, wup)

    fine_result, coarse_result = pl.pallas_call(
        spread_kernel,
        name="spread",
        out_shape=(jax.ShapeDtypeStruct((CAP, DF), bf16), jax.ShapeDtypeStruct((PCAP, DC), bf16)),
        in_specs=[sm] + [vm] * 9,
        out_specs=(hbm, hbm),
        scratch_shapes=[
            VMEM((CAP, DF), bf16),
            VMEM((TILE, DF), bf16),
            VMEM((BORDER, DC), bf16),
            dma((TILES,)),
            dma((2,)),
        ],
        compiler_params=params(20),
    )(meta, res, lifted, incoming, h2, parents, wpool, gc, cexp, cred)
    return fine_result, coarse_result


def solution(mesh):
    rows = P(AXES, None)
    in_specs = (rows, P(), P(AXES)) + (P(),) * 11
    return jax.shard_map(body, mesh=mesh, in_specs=in_specs, out_specs=(rows, rows), check_vma=False)
```

```python
import jax
import jax.numpy as jnp
from jax import lax
from jax.experimental import pallas as pl
from jax.experimental.pallas import tpu as pltpu
from jax.sharding import PartitionSpec as P

DF = 256
DC = 512
FF = 1024
FC = 2048
HD = 32
SPAN = 128
DIL = 4
WIN = 32
PCAP = 768
BORDER = 288
CAP = 6144
TILE = 512
TILES = CAP // TILE
NG = 4
LOCAL = PCAP + BORDER
STEP = 528
SLOTS = LOCAL + STEP
XROWS = SPAN + 5632 + SPAN
TAIL = 144
POOLW = 192
SPREADW = 256
GANG = 4
GAP = 1400
BSTEP = 144
EPS = 1e-5
AXES = ("zhi", "zlo")

COUNT, LOW, HIGH, BASE, EARLY, FIRST = 0, 1, 2, 3, 4, 5
META = FIRST + TILES

VMEM = pltpu.VMEM
SMEM = pltpu.SMEM
bf16 = jnp.bfloat16
f32 = jnp.float32
i32 = jnp.int32


def dot(a, b):
    return jnp.dot(a, b, preferred_element_type=f32)


def norm(v, gain):
    c = v - jnp.mean(v, axis=-1, keepdims=True)
    s = jnp.mean(c * c, axis=-1, keepdims=True)
    return c * lax.rsqrt(s + EPS) * gain


def gelu(u):
    h = 0.5 * u
    a = 0.7978845608028654
    t = jnp.tanh(u * (a + (a * 0.044715) * (u * u)))
    return h + h * t


def place():
    return lax.axis_index(AXES)


def put_rows(ref, at, rows):
    for t in range(DF // 128):
        ref[t, at, :] = rows[:, t * 128 : (t + 1) * 128]


def get_rows(ref, at):
    return jnp.concatenate([ref[t, at, :] for t in range(DF // 128)], axis=1)


def lane_masks():
    lb = lax.broadcasted_iota(i32, (1, DF), 1) // HD

    def one(c):
        return jnp.where(c, 1.0, 0.0).astype(bf16)

    return one(lb % 2 == 0), one(lb % 2 == 1), one(lb % 4 < 2), one(lb % 4 >= 2), lb % 4 < 2


def attend_weights(qkv, group, limit):
    key = lax.broadcasted_iota(i32, (WIN, 1), 0) * DIL
    even, odd, low, high, first = lane_masks()
    zero = jnp.zeros((128, 128), bf16)
    weights = [None] * DIL
    for p in range(DIL // 2):
        qa, ka, _ = [qkv[2 * p * WIN : (2 * p + 1) * WIN, c * DF : (c + 1) * DF] for c in range(3)]
        qb, kb, _ = [qkv[(2 * p + 1) * WIN : (2 * p + 2) * WIN, c * DF : (c + 1) * DF] for c in range(3)]
        ab = qa * even + qb * odd
        ba = qb * even + qa * odd
        parts = [ab * low, ab * high, ba * low, ba * high]
        left = jnp.concatenate([v[:, :128] for v in parts], axis=0)
        right = jnp.concatenate([v[:, 128:] for v in parts], axis=0)
        queries = jnp.concatenate(
            [jnp.concatenate([left, zero], axis=1), jnp.concatenate([zero, right], axis=1)], axis=0
        )
        keys = jnp.concatenate([ka * even, ka * odd, kb * even, kb * odd], axis=0)
        o = lax.dot_general(keys, queries, (((1,), (1,)), ((), ())), preferred_element_type=f32)
        sa = jnp.where(first, o[0:32], o[32:64])
        sb = jnp.where(first, o[96:128], o[64:96])
        for r, s in ((2 * p, sa), (2 * p + 1, sb)):
            live = group * SPAN + r + key < limit
            s = jnp.where(live, s * (HD**-0.5), -1e30)
            e = jnp.exp(s - jnp.max(s, axis=0, keepdims=True))
            weights[r] = (e * (1.0 / jnp.sum(e, axis=0, keepdims=True))).astype(bf16)
    return jnp.concatenate(weights, axis=0)


def attend_values(weights, qkv):
    even, odd, _, _, _ = lane_masks()
    head = lax.broadcasted_iota(i32, (WIN, 128), 1) // HD
    zero = jnp.zeros((64, 128), bf16)
    out = [[None] * 2 for _ in range(DIL)]
    for t in range(2):
        turned = jnp.transpose(weights[:, t * 128 : (t + 1) * 128])
        v = qkv[:, 2 * DF + t * 128 : 2 * DF + (t + 1) * 128]
        values = jnp.concatenate(
            [jnp.concatenate([v[:64], zero], axis=1), jnp.concatenate([zero, v[64:]], axis=1)], axis=0
        )
        o = dot(jnp.concatenate([turned * even[:, :128], turned * odd[:, :128]], axis=0), values)
        for r in range(DIL):
            b = o[(r % 2) * 128 : (r % 2 + 1) * 128, (r // 2) * 128 : (r // 2 + 1) * 128]
            order = (0, 2, 1, 3) if r % 2 == 0 else (2, 0, 3, 1)
            a = b[order[0] * WIN : (order[0] + 1) * WIN]
            for h in range(1, 4):
                a = jnp.where(head == h, b[order[h] * WIN : (order[h] + 1) * WIN], a)
            out[r][t] = a
    return jnp.concatenate([jnp.concatenate(o, axis=1) for o in out], axis=0).astype(bf16)


def attention_stage(off, limit, gids, x, h1s, gain, wqkv, wout):
    starts = [SPAN - off + SPAN * g + r for g in gids for r in range(DIL)]
    xs = jnp.concatenate([get_rows(x, pl.ds(s, WIN, stride=DIL)) for s in starts], axis=0)
    qkv = dot(norm(xs, gain[...]).astype(bf16), wqkv[...]).astype(bf16)
    yield
    spans = [qkv[i * SPAN : (i + 1) * SPAN] for i in range(len(gids))]
    weights = []
    for v, g in zip(spans, gids):
        weights.append(attend_weights(v, g, limit))
        yield
    out = []
    for i in range(len(gids)):
        out.append(attend_values(weights[i], spans[i]))
        yield
    h1s[...] = xs + dot(jnp.concatenate(out, axis=0), wout[...])


def feed_stage(off, gids, h, h1s, gain, wexp, wred):
    acc = h1s[...]
    n = norm(acc, gain[...]).astype(bf16)
    yield
    width = FF // 2
    for c in range(2):
        u = dot(n, wexp[:, c * width : (c + 1) * width])
        yield
        u = gelu(u).astype(bf16)
        yield
        acc = acc + dot(u, wred[c * width : (c + 1) * width, :])
        yield
    h2 = acc.astype(bf16).astype(f32)
    starts = [SPAN - off + SPAN * g + r for g in gids for r in range(DIL)]
    for w, s in enumerate(starts):
        put_rows(h, pl.ds(s, WIN, stride=DIL), h2[w * WIN : (w + 1) * WIN])


def interleave(*stages):
    stages = list(stages)
    while stages:
        for s in list(stages):
            if next(s, stages) is stages:
                stages.remove(s)


def fine_kernel(counts, parent, feats, prev, nxt, parents, gain1, gain2, gainc, wqkv_in, wout_in, wexp_in, wred_in,
                wpool_in, cexp_in, cred_in, wup_in, meta, h2_out, pooled_out, res, lifted, x, h, h1s, sums, cnts, wqkv, wout, wexp, wred,
                wpool, cexp, cred, wup, sem):
    loads = [pltpu.make_async_copy(a, b, sem.at[i]) for i, (a, b) in enumerate(
        ((wqkv_in, wqkv), (wout_in, wout), (wexp_in, wexp), (wred_in, wred)))]
    for c in loads:
        c.start()
    device = place()
    count = counts[device]
    tiles = (count + TILE - 1) // TILE
    last = counts.shape[0] - 1
    fullest = jnp.maximum(counts[jnp.maximum(device - 1, 0)], counts[jnp.minimum(device + 1, last)])
    light = fullest >= count + GAP
    coarse_loads = [pltpu.make_async_copy(a, b, sem.at[4 + i]) for i, (a, b) in enumerate(
        ((wpool_in, wpool), (cexp_in, cexp), (cred_in, cred), (wup_in, wup)))]

    @pl.when(light)
    def _():
        for c in coarse_loads:
            c.start()

    def add(i, c):
        return c[0] + jnp.where(i < device, counts[i], 0), c[1] + counts[i]

    start, total = lax.fori_loop(0, counts.shape[0], add, (jnp.int32(0), jnp.int32(0)))
    off = lax.rem(start, SPAN)
    limit = total - start + off
    groups = (off + count + SPAN - 1) // SPAN
    base0 = PCAP * device - BORDER
    meta[COUNT] = count
    meta[LOW] = parent[0] - base0
    meta[HIGH] = parent[count - 1] - base0
    meta[BASE] = base0
    meta[EARLY] = jnp.where(light, 1, 0)
    for t in range(TILES):
        meta[FIRST + t] = parent[t * TILE] - base0

    put_rows(h, pl.ds(0, TAIL), prev[...].astype(f32))
    put_rows(h, pl.ds(SPAN + TAIL, SPAN), nxt[...].astype(f32))
    before = counts[jnp.maximum(device - 1, 0)] - SPAN
    skip = lax.rem(before, 16)
    for r in range(DIL):
        put_rows(x, pl.ds(r, WIN, stride=DIL), get_rows(h, pl.ds(skip + r, WIN, stride=DIL)))
    sums[...] = jnp.zeros_like(sums)
    cnts[...] = jnp.zeros_like(cnts)

    def widen(t, _):
        r = pl.multiple_of(t * TILE, TILE)
        put_rows(x, pl.ds(SPAN + r, TILE), feats[pl.ds(r, TILE), :].astype(f32))
        return 0

    lax.fori_loop(0, tiles, widen, 0)
    for r in range(DIL):
        put_rows(x, pl.ds(SPAN + count + r, WIN, stride=DIL), get_rows(h, pl.ds(SPAN + TAIL + r, WIN, stride=DIL)))

    def gids(t):
        return [jnp.minimum(NG * t + g, groups - 1) for g in range(NG)]

    def attention(t):
        return attention_stage(off, limit, gids(t), x, h1s, gain1, wqkv, wout)

    def feed(t):
        return feed_stage(off, gids(t), h, h1s, gain2, wexp, wred)

    loads[0].wait()
    loads[1].wait()
    interleave(attention(0))
    loads[2].wait()
    loads[3].wait()

    def pool_stage(t):
        r = pl.multiple_of(t * TILE, TILE)
        row = lax.broadcasted_iota(i32, (TILE, 1), 0) + r
        rows = jnp.where(row < count, get_rows(h, pl.ds(SPAN + r, TILE)), 0.0).astype(bf16)
        h2_out[pl.ds(r, TILE), :] = rows
        yield
        lane = lax.broadcasted_iota(i32, (1, TILE), 1) + r
        seg = jnp.where(lane < count, parents[pl.ds(t, 1), :] - base0, -1)
        base = pl.multiple_of(((parent[r] - base0) // 16) * 16, 16)
        slot = lax.broadcasted_iota(i32, (POOLW, TILE), 0) + base
        hot = jnp.where(slot == seg, 1.0, 0.0)
        tally = jnp.sum(hot, axis=1, keepdims=True)
        yield
        sums[pl.ds(base, POOLW), :] += dot(hot.astype(bf16), rows)
        cnts[pl.ds(base, POOLW), :] += jnp.broadcast_to(tally, (POOLW, 128))

    def pool(t, _):
        interleave(pool_stage(t))
        return 0

    def both(t, _):
        interleave(feed(t - 1), attention(t))
        return 0

    def all_three(t, _):
        interleave(pool_stage(t - 3), feed(t - 1), attention(t))
        return 0

    steps = (groups + NG - 1) // NG
    lax.fori_loop(1, jnp.minimum(steps, 3), both, 0)
    lax.fori_loop(3, steps, all_three, 0)
    interleave(feed(steps - 1))
    lax.fori_loop(jnp.maximum(steps - 3, 0), tiles, pool, 0)
    n = jnp.maximum(cnts[...], 1.0)
    pooled_out[...] = (sums[...] / jnp.concatenate([n, n], axis=1)).astype(bf16)

    @pl.when(light)
    def _():
        for c in coarse_loads:
            c.wait()
        coarse_parents(parent[0] - base0, parent[count - 1] - base0, pooled_out, wpool, gainc, cexp, cred, wup,
                       res, lifted)


def coarse_rows(pooled, wpool, gain, wexp, wred):
    c = dot(pooled, wpool[...])
    n = norm(c, gain[...]).astype(bf16)
    acc = c
    u = dot(n, wexp[:, 0:512])
    for k in range(FC // 512):
        hid = gelu(u).astype(bf16)
        if k < FC // 512 - 1:
            u = dot(n, wexp[:, (k + 1) * 512 : (k + 2) * 512])
        acc = acc + dot(hid, wred[k * 512 : (k + 1) * 512, :])
    return acc.astype(bf16)


def coarse_parents(first, last, pooled, wpool, gain, cexp, cred, wup, res, lifted):
    lifted[...] = jnp.zeros_like(lifted)
    low = pl.multiple_of((first // 16) * 16, 16)

    def coarse(i, _):
        at = pl.ds(pl.multiple_of(low + i * STEP, 16), STEP)
        r = coarse_rows(pooled[at, :], wpool, gain, cexp, cred)
        res[at, :] = r
        lifted[at, :] = dot(r, wup[...]).astype(bf16)
        return 0

    lax.fori_loop(0, (last - low) // STEP + 1, coarse, 0)


def coarse_kernel(meta, pooled, res_in, lifted_in, wpool, gain, cexp, cred, wup, res, lifted, sem):
    light = meta[EARLY] == 1

    @pl.when(light)
    def _():
        copies = [pltpu.make_async_copy(res_in, res, sem.at[0]), pltpu.make_async_copy(lifted_in, lifted, sem.at[1])]
        for c in copies:
            c.start()
        for c in copies:
            c.wait()

    @pl.when(jnp.logical_not(light))
    def _():
        coarse_parents(meta[LOW], meta[HIGH], pooled, wpool, gain, cexp, cred, wup, res, lifted)


def spread_kernel(meta, res, lifted, incoming, h2, parents, wpool, gain, cexp, cred,
                  fine_out, coarse_out, ob, zeros, border, sem_out, sem):
    count = meta[COUNT]
    tiles = (count + TILE - 1) // TILE
    first = meta[HIGH] - BORDER + 1
    whole = PCAP - BORDER

    def rows_of(t):
        return pl.ds(pl.multiple_of(t * TILE, TILE), TILE)

    def copy_out(t):
        return pltpu.make_async_copy(ob.at[rows_of(t)], fine_out.at[rows_of(t)], sem_out.at[t])

    def copy_zero(t):
        return pltpu.make_async_copy(zeros, fine_out.at[rows_of(t)], sem_out.at[t])

    upper = pltpu.make_async_copy(res.at[pl.ds(BORDER, whole)], coarse_out.at[pl.ds(0, whole)], sem.at[0])
    upper.start()
    zeros[...] = jnp.zeros_like(zeros)

    def clear(t, _):
        copy_zero(t).start()
        return 0

    lax.fori_loop(tiles, TILES, clear, 0)

    def spread(t):
        r = pl.multiple_of(t * TILE, TILE)
        lane = lax.broadcasted_iota(i32, (1, TILE), 1) + r
        base = pl.multiple_of((meta[FIRST + t] // 16) * 16, 16)
        seg = jnp.where(lane < count, parents[pl.ds(t, 1), :] - (meta[BASE] + base), -1)
        col = jnp.transpose(jnp.broadcast_to(seg.astype(f32), (8, TILE)))[:, 0:1]
        slot = lax.broadcasted_iota(i32, (TILE, SPREADW), 1).astype(f32).astype(bf16)
        hot = jnp.where(slot == col.astype(bf16), jnp.ones((), bf16), jnp.zeros((), bf16))
        up = dot(hot, lifted[pl.ds(base, SPREADW), :])
        ob[pl.ds(r, TILE), :] = (h2[pl.ds(r, TILE), :].astype(f32) + up).astype(bf16)

    def several(i, _):
        for j in range(GANG):
            spread(jnp.minimum(i * GANG + j, tiles - 1))
        for j in range(GANG):
            @pl.when(i * GANG + j < tiles)
            def _():
                copy_out(i * GANG + j).start()
        return 0

    lax.fori_loop(0, (tiles + GANG - 1) // GANG, several, 0)

    def block(at, rows):
        row = lax.broadcasted_iota(i32, (rows, 1), 0) + (whole + at)
        new = coarse_rows(incoming[at : at + rows, :], wpool, gain, cexp, cred)
        old = res[PCAP + at : PCAP + at + rows, :]
        border[at : at + rows, :] = jnp.where(row >= first, new.astype(f32), old.astype(f32)).astype(bf16)

    many = first < whole + BSTEP

    @pl.when(many)
    def _():
        block(0, BORDER)

    @pl.when(jnp.logical_not(many))
    def _():
        border[0:BSTEP, :] = res[PCAP : PCAP + BSTEP, :]

    @pl.when(jnp.logical_and(jnp.logical_not(many), first < PCAP))
    def _():
        block(BSTEP, BSTEP)

    @pl.when(first >= PCAP)
    def _():
        border[BSTEP:BORDER, :] = res[PCAP + BSTEP : PCAP + BORDER, :]

    lower = pltpu.make_async_copy(border, coarse_out.at[pl.ds(whole, BORDER)], sem.at[1])
    lower.start()

    def end(t, _):
        copy_out(t).wait()
        return 0

    lax.fori_loop(0, tiles, end, 0)

    def end_zero(t, _):
        copy_zero(t).wait()
        return 0

    lax.fori_loop(tiles, TILES, end_zero, 0)
    upper.wait()
    lower.wait()


def ends_kernel(counts, feats, head, tail, sem):
    count = counts[place()]
    start = pl.multiple_of(((count - SPAN) // 16) * 16, 16)
    first = pltpu.make_async_copy(feats.at[pl.ds(0, SPAN)], head, sem.at[0])
    last = pltpu.make_async_copy(feats.at[pl.ds(start, TAIL)], tail, sem.at[1])
    first.start()
    last.start()
    first.wait()
    last.wait()


def passed_along(value, steps):
    count = lax.axis_size(AXES)
    first, last = max(0, -steps), min(count, count - steps)
    return lax.ppermute(value, AXES, [(s, s + steps) for s in range(first, last)])


def body(feats, counts, parent, gain1, wqkv, wout, gain2, wexp, wred, wpool, gainc, cexp, cred, wup):
    vm = pl.BlockSpec(memory_space=VMEM)
    sm = pl.BlockSpec(memory_space=SMEM)
    hbm = pl.BlockSpec(memory_space=pl.ANY)
    dma = pltpu.SemaphoreType.DMA
    def params(mib):
        return pltpu.CompilerParams(vmem_limit_bytes=mib * 1024 * 1024)


    def stay(*values):
        return [pltpu.with_memory_space_constraint(v, pltpu.HBM) for v in values]

    head, tail = pl.pallas_call(
        ends_kernel,
        name="ends",
        out_shape=(jax.ShapeDtypeStruct((SPAN, DF), bf16), jax.ShapeDtypeStruct((TAIL, DF), bf16)),
        in_specs=[sm, hbm],
        out_specs=(vm, vm),
        scratch_shapes=[dma((2,))],
    )(counts, *stay(feats))
    prev = passed_along(tail, 1)
    nxt = passed_along(head, -1)
    parents = parent.reshape(TILES, TILE)
    g1, g2, gc = gain1.reshape(1, DF), gain2.reshape(1, DF), gainc.reshape(1, DC)

    cold = stay(wpool, cexp, cred, wup)
    wpool, cexp, cred, wup = [pltpu.with_memory_space_constraint(w, VMEM) for w in (wpool, cexp, cred, wup)]

    meta, h2, pooled, res, lifted = pl.pallas_call(
        fine_kernel,
        name="fine",
        out_shape=(
            jax.ShapeDtypeStruct((META,), i32),
            jax.ShapeDtypeStruct((CAP, DF), bf16),
            jax.ShapeDtypeStruct((SLOTS, DF), bf16),
            jax.ShapeDtypeStruct((SLOTS, DC), bf16),
            jax.ShapeDtypeStruct((SLOTS, DF), bf16),
        ),
        in_specs=[sm, sm] + [vm] * 7 + [hbm] * 8,
        out_specs=(sm, vm, vm, vm, vm),
        scratch_shapes=[
            VMEM((DF // 128, XROWS, 128), f32),
            VMEM((DF // 128, XROWS, 128), f32),
            VMEM((NG * SPAN, DF), f32),
            VMEM((SLOTS, DF), f32),
            VMEM((SLOTS, 128), f32),
            VMEM((DF, 3 * DF), bf16),
            VMEM((DF, DF), bf16),
            VMEM((DF, FF), bf16),
            VMEM((FF, DF), bf16),
            VMEM((DF, DC), bf16),
            VMEM((DC, FC), bf16),
            VMEM((FC, DC), bf16),
            VMEM((DC, DF), bf16),
            dma((8,)),
        ],
        compiler_params=params(38),
    )(counts, parent, feats, prev, nxt, parents, g1, g2, gc, *stay(wqkv, wout, wexp, wred), *cold)

    incoming = passed_along(pooled[:BORDER], -1)

    res, lifted = pl.pallas_call(
        coarse_kernel,
        name="coarse",
        out_shape=(jax.ShapeDtypeStruct((SLOTS, DC), bf16), jax.ShapeDtypeStruct((SLOTS, DF), bf16)),
        in_specs=[sm, vm, hbm, hbm] + [vm] * 5,
        out_specs=(vm, vm),
        scratch_shapes=[dma((2,))],
        compiler_params=params(20),
    )(meta, pooled, res, lifted, wpool, gc, cexp, cred, wup)

    fine_result, coarse_result = pl.pallas_call(
        spread_kernel,
        name="spread",
        out_shape=(jax.ShapeDtypeStruct((CAP, DF), bf16), jax.ShapeDtypeStruct((PCAP, DC), bf16)),
        in_specs=[sm] + [vm] * 9,
        out_specs=(hbm, hbm),
        scratch_shapes=[
            VMEM((CAP, DF), bf16),
            VMEM((TILE, DF), bf16),
            VMEM((BORDER, DC), bf16),
            dma((TILES,)),
            dma((2,)),
        ],
        compiler_params=params(20),
    )(meta, res, lifted, incoming, h2, parents, wpool, gc, cexp, cred)
    return fine_result, coarse_result


def solution(mesh):
    rows = P(AXES, None)
    in_specs = (rows, P(), P(AXES)) + (P(),) * 11
    return jax.shard_map(body, mesh=mesh, in_specs=in_specs, out_specs=(rows, rows), check_vma=False)
```
